512 devices in a mesh: row: 32 (over y, z_lo, core), col: 16 (over z_hi, x).
Axes of the slice: x: 4, y: 4, z: 16 (z_hi: 4, z_lo: 4; z = z_hi * 4 + z_lo), core: 2. Of those that a mesh axis runs over, the one named last changes fastest.
Arguments:
- queries: bfloat16 [32768, 2048], P('row', 'col'), may hold values from -122 to 122
- key_vectors: bfloat16 [32768, 128], P(('col', 'row')), may hold values from -6.1 to 6.1
- value_vectors: bfloat16 [32768, 128], P(('col', 'row')), may hold values from -6 to 6
- block_mask: int32 [64, 64], replicated, may hold values from 0 to 1, as said below
Outputs:
- attended: bfloat16 [32768, 2048], P('row', 'col')
The draws below stay inside these ranges and needn't reach their ends.
Inputs may be any that keep to these rules, and one draw needn't show every extreme that they name: `block_mask`: query block i attends to key block j only when j <= i; every block attends to itself; a tile (r, c) lists at most 3 pairs, and the tiles that hold the diagonal list exactly 3.
All inputs are finite; a program needn't handle non-finite values.
Results may differ from the reference program's by a relative error of at most 0.015.
Values may be sent and summed in bfloat16 or wider, within the bound.
A program may use at most 192 MiB of HBM per device.

```python
import jax
import jax.numpy as jnp
from jax import lax

HEAD_DIM = 128
BLOCK = 512
QB = 2
SLOTS = 3
KB = 4
NB = 64
SEQ = 32768
FEAT = 2048
N_ROW = 32
N_COL = 16


def shared_keys(key):
    base_keys = jax.random.normal(jax.random.fold_in(key, 11), (SEQ, HEAD_DIM), jnp.float32)
    return jnp.clip(base_keys, -6.0, 6.0)


def draw_key_vectors(key, part):
    base_keys = shared_keys(key)
    return base_keys.astype(jnp.bfloat16)


def draw_queries(key, part):
    key = jax.random.fold_in(key, 3)
    drawn = jnp.clip(jax.random.normal(key, (SEQ, FEAT), jnp.float32), -6.0, 6.0)
    return drawn.astype(jnp.bfloat16)


def draw_block_mask(key, part):
    key = jax.random.fold_in(key, 7)
    first_key, second = jax.random.split(key)
    raw_scores = jax.random.randint(first_key, (N_ROW, N_COL, QB * KB), 0, 1 << 20) * 64 + jnp.arange(QB * KB, dtype=jnp.int32)
    rank_within = jnp.sum((raw_scores[:, :, None, :] < raw_scores[:, :, :, None]).astype(jnp.int32), axis=-1)
    pair_count = jax.random.randint(second, (N_ROW, N_COL, 1), 0, SLOTS + 1)
    row_ids = jnp.arange(N_ROW, dtype=jnp.int32)[:, None, None]
    col_ids = jnp.arange(N_COL, dtype=jnp.int32)[None, :, None]
    lower_tile = (col_ids + 1) * KB <= row_ids * QB
    picked = jnp.logical_and(rank_within < pair_count, lower_tile)
    tile_grid = picked.reshape(N_ROW, N_COL, QB, KB).transpose(0, 2, 1, 3).reshape(NB, NB)
    q_block = jnp.arange(NB, dtype=jnp.int32)[:, None]
    k_block = jnp.arange(NB, dtype=jnp.int32)[None, :]
    below = jnp.logical_and(q_block == k_block + 1, q_block % QB != 0)
    near = jnp.logical_or(q_block == k_block, below)
    return jnp.logical_or(tile_grid, near).astype(jnp.int32)


def shard_levels(stream_key, extent, cuts, smallest, high):
    factor_of = 1.0
    for axis_at, blocks in cuts:
        draws = jax.random.uniform(jax.random.fold_in(jax.random.fold_in(stream_key, 6), axis_at), (blocks,), jnp.float32, smallest / len(cuts), high / len(cuts))
        factor_of = factor_of * jnp.repeat(jnp.exp(draws), extent[axis_at] // blocks).reshape((-1,) + (1,) * (len(extent) - 1 - axis_at))
    return factor_of


def normal_values(stream_key, dims, deviation, limit, pieces=(), kind=jnp.bfloat16):
    entries = jax.random.normal(stream_key, dims, jnp.float32) * deviation
    if len(pieces) > 0:
        entries = shard_levels(stream_key, dims, pieces, -0.22, 0.18) * entries
    return jnp.clip(entries, min=-limit, max=limit).astype(kind)


def setup_inputs(seed: int = 0) -> dict:
    arg_keys = jax.random.split(jax.random.key(seed), 5)
    queries = draw_queries(jax.random.fold_in(arg_keys[4], 71), 0)
    key_vectors = draw_key_vectors(jax.random.fold_in(arg_keys[4], 71), 0)
    value_vectors = normal_values(arg_keys[2], (SEQ, HEAD_DIM), 1.0, 6.0, ((0, 512),))
    block_mask = draw_block_mask(jax.random.fold_in(arg_keys[4], 71), 0)
    return dict(queries=queries, key_vectors=key_vectors, value_vectors=value_vectors, block_mask=block_mask)


NEG_FILL = -1e30


def tile_terms(queries, key_stretch, value_stretch, tile_flags, row_start, key_start):
    row_count = queries.shape[0]
    head_width = key_stretch.shape[1]
    head_count = queries.shape[1] // head_width
    q_blocks = tile_flags.shape[0]
    k_blocks = tile_flags.shape[1]
    block_len = row_count // q_blocks
    pair_count = q_blocks * k_blocks
    score_scale = head_width ** -0.5
    running = jnp.cumsum(tile_flags.reshape(pair_count)).astype(jnp.int32)
    shaped = queries.reshape(row_count, head_count, head_width)
    group_size = min(head_count, 4)
    maxima = jnp.full((head_count, row_count), NEG_FILL, jnp.float32)
    totals = jnp.zeros((head_count, row_count), jnp.float32)
    accumulated = jnp.zeros((row_count, head_count, head_width), jnp.float32)
    for slot_index in range(SLOTS):
        position = jnp.minimum(jnp.sum((running <= slot_index).astype(jnp.int32)), pair_count - 1)
        active = running[pair_count - 1] > slot_index
        qstart = ((position // k_blocks) * block_len).astype(jnp.int32)
        kstart = ((position % k_blocks) * block_len).astype(jnp.int32)
        kblock = lax.dynamic_slice_in_dim(key_stretch, kstart, block_len, 0).astype(jnp.float32)
        vblock = lax.dynamic_slice_in_dim(value_stretch, kstart, block_len, 0).astype(jnp.float32)
        query_pos = row_start + qstart + jnp.arange(block_len, dtype=jnp.int32)
        key_pos = key_start + kstart + jnp.arange(block_len, dtype=jnp.int32)
        allowed = jnp.logical_and(key_pos[None, :] <= query_pos[:, None], active)
        for head_first in range(0, head_count, group_size):
            query_part = lax.dynamic_slice_in_dim(shaped[:, head_first:head_first + group_size], qstart, block_len, 0).astype(jnp.float32)
            scores = jnp.einsum("qhd,kd->hqk", query_part, kblock) * score_scale
            scores = jnp.where(allowed[None], scores, NEG_FILL)
            start_pair = (jnp.int32(head_first), qstart)
            old_max = lax.dynamic_slice(maxima, start_pair, (group_size, block_len))
            new_max = jnp.maximum(old_max, jnp.max(scores, axis=-1))
            factor = jnp.exp(old_max - new_max)
            unnormed = jnp.where(allowed[None], jnp.exp(scores - new_max[:, :, None]), 0.0)
            old_tot = lax.dynamic_slice(totals, start_pair, (group_size, block_len))
            new_tot = old_tot * factor + jnp.sum(unnormed, axis=-1)
            weights = unnormed.astype(jnp.bfloat16).astype(jnp.float32)
            mixed_values = jnp.einsum("hqk,kd->qhd", weights, vblock)
            acc_start = (qstart, jnp.int32(head_first), jnp.int32(0))
            old_acc = lax.dynamic_slice(accumulated, acc_start, (block_len, group_size, head_width))
            new_acc = old_acc * factor.T[:, :, None] + mixed_values
            maxima = lax.dynamic_update_slice(maxima, new_max, start_pair)
            totals = lax.dynamic_update_slice(totals, new_tot, start_pair)
            accumulated = lax.dynamic_update_slice(accumulated, new_acc, acc_start)
    return maxima, totals, accumulated.reshape(row_count, head_count * head_width)


def reference(queries, key_vectors, value_vectors, block_mask):
    row_span = QB * BLOCK
    stretch_len = KB * BLOCK

    def one_row(row_index):
        query_rows = lax.dynamic_slice_in_dim(queries, row_index * row_span, row_span, 0)

        def one_tile(col_index):
            tile_flags = lax.dynamic_slice(block_mask, (row_index * QB, col_index * KB), (QB, KB))
            key_stretch = lax.dynamic_slice_in_dim(key_vectors, col_index * stretch_len, stretch_len, 0)
            value_stretch = lax.dynamic_slice_in_dim(value_vectors, col_index * stretch_len, stretch_len, 0)
            return tile_terms(query_rows, key_stretch, value_stretch, tile_flags, row_index * row_span, col_index * stretch_len)

        maxima, totals, accumulated = lax.map(one_tile, jnp.arange(N_COL, dtype=jnp.int32))
        global_max = jnp.max(maxima, axis=0)
        weight = jnp.exp(maxima - global_max[None])
        spread = jnp.repeat(jnp.transpose(weight, (0, 2, 1)), HEAD_DIM, axis=2)
        shares_bf = (accumulated * spread).astype(jnp.bfloat16)
        numerator = jnp.sum(shares_bf.astype(jnp.float32), axis=0)
        denominator = jnp.sum(totals * weight, axis=0)
        return (numerator / jnp.repeat(denominator.T, HEAD_DIM, axis=1)).astype(jnp.bfloat16)

    result_rows = lax.map(one_row, jnp.arange(N_ROW, dtype=jnp.int32))
    return result_rows.reshape(SEQ, FEAT)
```

```python
import jax
import jax.numpy as jnp
from jax import lax
from jax.experimental import pallas as pl
from jax.experimental.pallas import tpu as pltpu
from jax.sharding import PartitionSpec as P

HEAD_DIM = 128
BLOCK = 512
SLOTS = 3
RING = 4
ZRING = 16
NSLOT = SLOTS * RING
PIECE = 128
HALF = 64
SUMROWS = 16
NEG_FILL = -1e30
EXP_SCALE = 1.4426950408889634 * HEAD_DIM**-0.5
MESH = pl.DeviceIdType.MESH
f32 = jnp.float32
bf16 = jnp.bfloat16


def dot(a, b, dims):
    return lax.dot_general(a, b, (dims, ((), ())), preferred_element_type=f32)


def kernel(
    mask_ref,
    q_ref,
    k_ref,
    v_ref,
    o_ref,
    qg,
    kv,
    half,
    scores,
    state,
    maxima,
    osend,
    orecv,
    ssend,
    srecv,
    info_i,
    info_j,
    info_prev,
    info_thr,
    last,
    own_sem,
    half_sem,
    q_sem,
    ya_sem,
    yb_sem,
    za_send,
    za_recv,
    zb_send,
    zb_recv,
    sib_sem,
    o_sem,
    s_sem,
):
    r = lax.axis_index("row")
    c = lax.axis_index("col")
    core = lax.rem(r, 2)
    zl = lax.rem(r // 2, RING)
    y = r // 8
    x = lax.rem(c, RING)
    z = (c // RING) * RING + zl

    def at_x(d):
        return (r, (c // RING) * RING + lax.rem(x + d, RING))

    def at_y(d):
        return (lax.rem(y + d, RING) * 8 + lax.rem(r, 8), c)

    def at_z(d):
        t = lax.rem(z + d + ZRING, ZRING)
        return (y * 8 + lax.rem(t, RING) * 2 + core, (t // RING) * RING + x)

    sibling = (r + 1 - 2 * core, c)

    def remote(src, dst, send, recv, device):
        return pltpu.make_async_remote_copy(
            src_ref=src, dst_ref=dst, send_sem=send, recv_sem=recv, device_id=device, device_id_type=MESH
        )

    def drain(view, sem):
        pltpu.make_async_copy(view, view, sem).wait()

    barrier = pltpu.get_barrier_semaphore()
    partners = [sibling, at_z(1), at_z(-1)] + [at_x(d) for d in (1, 2, 3)] + [at_y(d) for d in (1, 2, 3)]
    for partner in partners:
        pl.semaphore_signal(barrier, inc=1, device_id=partner, device_id_type=MESH)
    pl.semaphore_wait(barrier, len(partners))

    @pl.when(core == 0)
    def _():
        remote(v_ref, half, half_sem.at[0], half_sem.at[1], sibling).start()

    @pl.when(core == 1)
    def _():
        remote(k_ref, half, half_sem.at[0], half_sem.at[1], sibling).start()

    own = pltpu.make_async_copy(q_ref, qg.at[0], own_sem)
    own.start()
    q_copies = [remote(q_ref, qg.at[RING - d], q_sem.at[0, d], q_sem.at[1, RING - d], at_x(d)) for d in (1, 2, 3)]
    for copy in q_copies:
        copy.start()

    remote(v_ref, half, half_sem.at[0], half_sem.at[1], sibling).wait()

    @pl.when(core == 0)
    def _():
        kv[0, z, y] = jnp.concatenate([k_ref[...], half[...]], axis=0)

    @pl.when(core == 1)
    def _():
        kv[1, z, y] = jnp.concatenate([half[...], v_ref[...]], axis=0).astype(f32).T.astype(bf16)

    lower, upper = pl.ds(0, HALF), pl.ds(HALF, HALF)

    def slab(t):
        return kv.at[core, t, :, lower]

    def piece(t):
        return kv.at[core, t, y, upper]

    def send_slab(t, direction, step):
        remote(
            slab(t), slab(t), za_send.at[direction], za_recv.at[direction, step], at_z(1 - 2 * direction)
        ).start()

    def send_piece(t, direction, step):
        remote(
            piece(t), piece(t), zb_send.at[direction], zb_recv.at[direction, step], at_z(1 - 2 * direction)
        ).start()

    def spread_piece(t):
        for d in (1, 2, 3):
            remote(piece(t), piece(t), yb_sem.at[0], yb_sem.at[1], at_y(d)).start()

    def share_slab(t):
        remote(slab(t), slab(t), sib_sem.at[0], sib_sem.at[1], sibling).start()

    a_copies = [
        remote(kv.at[core, z, y, lower], kv.at[core, z, y, lower], ya_sem.at[0, d], ya_sem.at[1, d], at_y(d))
        for d in (1, 2, 3)
    ]
    for copy in a_copies:
        copy.start()
    for direction in (0, 1):
        send_piece(z, direction, 1)
    spread_piece(z)

    def wait_slab(t, direction, step):
        drain(slab(t), za_recv.at[direction, step])

    def wait_piece(t, direction, step):
        drain(piece(t), zb_recv.at[direction, step])

    for d in (1, 2, 3):
        from_y = lax.rem(y + RING - d, RING)
        drain(kv.at[core, z, from_y, lower], ya_sem.at[1, d])
    for direction in (0, 1):
        send_slab(z, direction, 1)
    share_slab(z)

    for i in (0, 1):
        last[i] = jnp.int32(NSLOT)
    for b in range(RING):
        count = jnp.int32(0)
        found_i = [jnp.int32(0)] * SLOTS
        found_j = [jnp.int32(0)] * SLOTS
        for i in (0, 1):
            for j in range(RING):
                flag = mask_ref[2 * r + i, (b * RING + x) * RING + j]
                for s in range(SLOTS):
                    here = flag * jnp.where(count == s, 1, 0)
                    found_i[s] = found_i[s] + here * i
                    found_j[s] = found_j[s] + here * j
                count = count + flag
        for s in range(SLOTS):
            t = b * SLOTS + s
            active = count > s
            i, j = found_i[s], found_j[s]
            info_i[t] = i
            info_j[t] = j
            info_prev[t] = jnp.where(i == 0, last[0], last[1])
            info_thr[t] = jnp.where(2 * r + i == (b * RING + x) * RING + j, 0, BLOCK)
            last[0] = jnp.where(jnp.logical_and(active, i == 0), t, last[0])
            last[1] = jnp.where(jnp.logical_and(active, i == 1), t, last[1])
    state[NSLOT] = jnp.zeros(state.shape[1:], f32)
    maxima[NSLOT] = jnp.full(maxima.shape[1:], NEG_FILL, f32)

    def ring_step(step, forward_plus, forward_minus, minus):
        plus_t = lax.rem(z - step + ZRING, ZRING)
        minus_t = lax.rem(z + step, ZRING)
        wait_slab(plus_t, 0, step)
        if forward_plus:
            send_slab(plus_t, 0, step + 1)
        if minus:
            wait_slab(minus_t, 1, step)
            if forward_minus:
                send_slab(minus_t, 1, step + 1)
        wait_piece(plus_t, 0, step)
        if forward_plus:
            send_piece(plus_t, 0, step + 1)
        if minus:
            wait_piece(minus_t, 1, step)
            if forward_minus:
                send_piece(minus_t, 1, step + 1)
        spread_piece(plus_t)
        share_slab(plus_t)
        if minus:
            spread_piece(minus_t)
            share_slab(minus_t)

    def ring_body(step, carry):
        ring_step(step, True, True, True)
        return carry

    lax.fori_loop(1, ZRING // 2 - 1, ring_body, 0)
    ring_step(ZRING // 2 - 1, True, False, True)
    ring_step(ZRING // 2, False, False, False)

    drain(kv.at[core, :, pl.ds(0, 3), upper], yb_sem.at[1])
    uppers = remote(
        kv.at[core, :, :, upper], kv.at[core, :, :, upper], sib_sem.at[2], sib_sem.at[3], sibling
    )
    uppers.start()
    drain(kv.at[1 - core, :, :, lower], sib_sem.at[1])
    own.wait()
    for d in (1, 2, 3):
        q_copies[d - 1].wait_recv()
    drain(kv.at[1 - core, :, :, upper], sib_sem.at[3])

    ones = jnp.ones((SUMROWS, BLOCK), bf16)
    offset = lax.broadcasted_iota(jnp.int32, (BLOCK, BLOCK), 0) - lax.broadcasted_iota(
        jnp.int32, (BLOCK, BLOCK), 1
    )

    def score(head, t):
        b4 = (t // SLOTS) * RING
        keys = jnp.concatenate([kv[0, b4 + n, info_j[t]] for n in range(RING)], axis=0)
        return dot(keys, qg[head, info_i[t]], ((1,), (1,)))

    def soften(t, s, masked):
        b4 = (t // SLOTS) * RING
        prev = info_prev[t]
        if masked:
            s = jnp.where(offset <= info_thr[t], s, NEG_FILL)
        old_max = maxima[prev]
        new_max = jnp.maximum(old_max, jnp.max(s, axis=0, keepdims=True))
        factor = jnp.exp2((old_max - new_max) * EXP_SCALE)
        weights = jnp.exp2((s - new_max) * EXP_SCALE).astype(bf16)
        values = jnp.concatenate([kv[1, b4 + n, info_j[t]] for n in range(RING)], axis=1)
        values = jnp.concatenate([values, ones], axis=0)
        maxima[t] = new_max
        state[t] = state[prev] * factor + dot(values, weights, ((1,), (0,)))

    def stretch(head, b, masked):
        for s in range(SLOTS):
            t = b * SLOTS + s
            following = jnp.minimum(t + 1, NSLOT - 1)
            scores[(s + 1) % SLOTS] = score(head, following)
            soften(t, scores[s], masked)

    def head_body(n, carry):
        head = lax.rem(n + 1, RING)
        scores[0] = score(head, 0)

        def stretch_body(b, inner):
            stretch(head, b, False)
            return inner

        lax.fori_loop(0, y, stretch_body, 0)

        @pl.when(x <= zl)
        def _():
            stretch(head, y, True)

        for i in (0, 1):
            final = state[last[i]]
            osend[head, i] = final[:HEAD_DIM].astype(bf16)
            ssend[head, pl.ds(2 * i, 1)] = maxima[last[i]]
            ssend[head, pl.ds(2 * i + 1, 1)] = final[HEAD_DIM : HEAD_DIM + 1]

        @pl.when(n < RING - 1)
        def _():
            slot = RING - head
            remote(osend.at[head], orecv.at[slot - 1], o_sem.at[0, head], o_sem.at[1, slot], at_x(head)).start()
            remote(ssend.at[head], srecv.at[slot - 1], s_sem.at[0, head], s_sem.at[1, slot], at_x(head)).start()

        return carry

    lax.fori_loop(0, RING, head_body, 0)

    for d in (1, 2, 3):
        drain(orecv.at[d - 1], o_sem.at[1, d])
        drain(srecv.at[d - 1], s_sem.at[1, d])
    for i in (0, 1):
        stats = [ssend[0]] + [srecv[n] for n in range(RING - 1)]
        parts = [osend[0, i]] + [orecv[n, i] for n in range(RING - 1)]
        tops = [a[2 * i : 2 * i + 1] for a in stats]
        totals = [a[2 * i + 1 : 2 * i + 2] for a in stats]
        top = jnp.maximum(jnp.maximum(tops[0], tops[1]), jnp.maximum(tops[2], tops[3]))
        shares = [jnp.exp2((a - top) * EXP_SCALE) for a in tops]
        denominator = sum(a * b for a, b in zip(shares, totals))
        out = sum(p.astype(f32) * (a / denominator) for p, a in zip(parts, shares))
        o_ref[pl.ds(i * BLOCK, BLOCK)] = out.T.astype(bf16)

    for d in (1, 2, 3):
        q_copies[d - 1].wait_send()
        a_copies[d - 1].wait_send()
        drain(osend.at[d], o_sem.at[0, d])
        drain(ssend.at[d], s_sem.at[0, d])
    drain(kv.at[core, :, pl.ds(0, 3), upper], yb_sem.at[0])
    drain(kv.at[core, pl.ds(0, 8), :, lower], za_send.at[0])
    drain(kv.at[core, pl.ds(0, 7), :, lower], za_send.at[1])
    drain(kv.at[core, pl.ds(0, 8), y, upper], zb_send.at[0])
    drain(kv.at[core, pl.ds(0, 7), y, upper], zb_send.at[1])
    drain(kv.at[core, :, :, lower], sib_sem.at[0])
    uppers.wait_send()


def body(queries, key_vectors, value_vectors, block_mask):
    rows, width = queries.shape
    vmem = pl.BlockSpec(memory_space=pltpu.VMEM)
    dma = pltpu.SemaphoreType.DMA
    return pl.pallas_call(
        kernel,
        out_shape=jax.ShapeDtypeStruct((rows, width), bf16),
        in_specs=[
            pl.BlockSpec(memory_space=pltpu.SMEM),
            pl.BlockSpec(memory_space=pl.ANY),
            vmem,
            vmem,
        ],
        out_specs=vmem,
        scratch_shapes=[
            pltpu.VMEM((RING, 2, BLOCK, HEAD_DIM), bf16),
            pltpu.VMEM((2, ZRING, RING, PIECE, HEAD_DIM), bf16),
            pltpu.VMEM((HALF, HEAD_DIM), bf16),
            pltpu.VMEM((SLOTS, BLOCK, BLOCK), f32),
            pltpu.VMEM((NSLOT + 1, HEAD_DIM + SUMROWS, BLOCK), f32),
            pltpu.VMEM((NSLOT + 1, 1, BLOCK), f32),
            pltpu.VMEM((RING, 2, HEAD_DIM, BLOCK), bf16),
            pltpu.VMEM((RING - 1, 2, HEAD_DIM, BLOCK), bf16),
            pltpu.VMEM((RING, 8, BLOCK), f32),
            pltpu.VMEM((RING - 1, 8, BLOCK), f32),
            pltpu.SMEM((NSLOT,), jnp.int32),
            pltpu.SMEM((NSLOT,), jnp.int32),
            pltpu.SMEM((NSLOT,), jnp.int32),
            pltpu.SMEM((NSLOT,), jnp.int32),
            pltpu.SMEM((2,), jnp.int32),
            dma,
            dma((2,)),
            dma((2, RING)),
            dma((2, RING)),
            dma((2,)),
            dma((2,)),
            dma((2, ZRING)),
            dma((2,)),
            dma((2, ZRING)),
            dma((4,)),
            dma((2, RING)),
            dma((2, RING)),
        ],
        compiler_params=pltpu.CompilerParams(
            collective_id=0, has_side_effects=True, vmem_limit_bytes=48 * 2**20
        ),
    )(block_mask, queries.reshape(2, BLOCK, width), key_vectors, value_vectors)


def solution(mesh):
    placed = (P("row", "col"), P(("col", "row"), None), P(("col", "row"), None), P())
    return jax.shard_map(body, mesh=mesh, in_specs=placed, out_specs=P("row", "col"), check_vma=False)
```

```python
import functools

import jax
import jax.numpy as jnp
from jax import lax
from jax.experimental import pallas as pl
from jax.experimental.pallas import tpu as pltpu
from jax.sharding import PartitionSpec as P

HEAD_DIM = 128
BLOCK = 512
SLOTS = 3
RING = 4
ZRING = 16
NSLOT = SLOTS * RING
PIECE = 128
HALF = 64
SUMROWS = 16
HERE = 8
LAST = 7
ROUNDS = 4
MESSAGES = 6
NEG_FILL = -1e30
NO_CAP = 3e38
EXP_SCALE = 1.4426950408889634 * HEAD_DIM**-0.5
MESH = pl.DeviceIdType.MESH
f32 = jnp.float32
bf16 = jnp.bfloat16


def dot(a, b, dims):
    return lax.dot_general(a, b, (dims, ((), ())), preferred_element_type=f32)


def kernel(
    mask_hbm,
    q_ref,
    k_ref,
    v_ref,
    o_ref,
    mask_ref,
    qg,
    kv,
    raw,
    scores,
    cap,
    near0,
    near1,
    state,
    maxima,
    osend,
    orecv,
    oin,
    ssend,
    srecv,
    sin,
    info_i,
    info_j,
    info_prev,
    info_diag,
    last,
    own_sem,
    near_sem,
    raw_sem,
    far_sem,
    q_sem,
    yb_send,
    yb_recv,
    z_send,
    z_recv,
    sib_send,
    sib_recv,
    o_sem,
    s_sem,
):
    r = lax.axis_index("row")
    c = lax.axis_index("col")
    core = lax.rem(r, 2)
    zl = lax.rem(r // 2, RING)
    y = r // 8
    x = lax.rem(c, RING)
    z = (c // RING) * RING + zl
    parity, plane = lax.rem(y, 2), y // 2

    def at_x(d):
        return (r, (c // RING) * RING + lax.rem(x + d, RING))

    def at_y(d):
        return (lax.rem(y + d, RING) * 8 + lax.rem(r, 8), c)

    def at_z(d):
        t = lax.rem(z + d + ZRING, ZRING)
        return (y * 8 + lax.rem(t, RING) * 2 + core, (t // RING) * RING + x)

    sibling = (r + 1 - 2 * core, c)
    far = at_y(2)
    far_sibling = (far[0] + 1 - 2 * core, c)

    def remote(src, dst, send, recv, device):
        return pltpu.make_async_remote_copy(
            src_ref=src, dst_ref=dst, send_sem=send, recv_sem=recv, device_id=device, device_id_type=MESH
        )

    def drain(view, sem):
        pltpu.make_async_copy(view, view, sem).wait()

    own_k = pltpu.make_async_copy(k_ref, kv.at[HERE, parity, core, 0, plane], own_sem.at[0])
    own_v = pltpu.make_async_copy(v_ref, raw.at[0, core], own_sem.at[1])
    own_q = pltpu.make_async_copy(q_ref, qg.at[0], own_sem.at[2])
    own_mask = pltpu.make_async_copy(mask_hbm, mask_ref, own_sem.at[3])
    for copy in (own_k, own_v, own_q, own_mask):
        copy.start()

    barrier = pltpu.get_barrier_semaphore()
    partners = [sibling, far_sibling] + [at_z(d) for d in (1, -1, 2, -2)]
    partners += [at_x(d) for d in (1, 2, 3)] + [at_y(d) for d in (1, 2, 3)]
    for partner in partners:
        pl.semaphore_signal(barrier, inc=1, device_id=partner, device_id_type=MESH)
    pl.semaphore_wait(barrier, len(partners))

    first_copies = [
        remote(k_ref, kv.at[HERE, parity, core, 0, plane], far_sem.at[0], far_sem.at[1], far),
        remote(v_ref, raw.at[0, core], raw_sem.at[0, 0], raw_sem.at[1, 0], sibling),
        remote(v_ref, raw.at[1, core], raw_sem.at[0, 1], raw_sem.at[1, 1], far),
        remote(v_ref, raw.at[1, core], raw_sem.at[0, 2], raw_sem.at[1, 2], far_sibling),
    ]
    for copy in first_copies:
        copy.start()
    q_copies = [remote(q_ref, qg.at[RING - d], q_sem.at[0, d], q_sem.at[1, RING - d], at_x(d)) for d in (1, 2, 3)]
    for copy in q_copies:
        copy.start()

    def slab(stream, o):
        return kv.at[HERE + o, parity, core, stream % 2, plane if stream < 2 else 1 - plane]

    def send_z(stream, o, hop):
        remote(
            slab(stream, o), slab(stream, o - hop), z_send.at[stream], z_recv.at[stream, HERE + o - hop], at_z(hop)
        ).start()

    def wait_z(stream, o):
        drain(slab(stream, o), z_recv.at[stream, HERE + o])

    def pieces(first, count, from_y):
        return kv.at[pl.ds(HERE + first, count), lax.rem(from_y, 2), core, :, from_y // 2]

    def spread(n, way, first, count):
        for d in (1, 3):
            view = pieces(first, count, y)
            remote(view, view, yb_send, yb_recv.at[n, way, d // 2], at_y(d)).start()

    def gathered(n, way, first, count):
        for d in (1, 3):
            drain(pieces(first, count, lax.rem(y + RING - d, RING)), yb_recv.at[n, way, d // 2])

    def shared(first, count, of_core):
        return kv.at[pl.ds(HERE + first, count), :, of_core]

    def share(n, way, first, count):
        view = shared(first, count, core)
        remote(view, view, sib_send, sib_recv.at[n, way], sibling).start()

    def arrivals(n):
        if n == 0:
            return [(0, 0, 1)]
        return [(0, -2 * n, 2), (1, 2 * n - 1, 2 if n < ROUNDS else 1)]

    own_k.wait()
    for hop in (2, -2, 1, -1):
        send_z(0, 0, hop)
    own_v.wait()
    drain(raw.at[0, 1 - core], raw_sem.at[1, 0])
    own_turned = raw[0].reshape(PIECE, HEAD_DIM).astype(f32).T.astype(bf16)
    for i in (0, 1):

        @pl.when(core == i)
        def _():
            kv[HERE, parity, i, 1, plane] = own_turned[i * HALF : (i + 1) * HALF]

    for hop in (2, -2, 1, -1):
        send_z(1, 0, hop)
    drain(kv.at[HERE, parity, core, 0, 1 - plane], far_sem.at[1])
    for hop in (2, -2, 1, -1):
        send_z(2, 0, hop)
    drain(raw.at[1, core], raw_sem.at[1, 1])
    drain(raw.at[1, 1 - core], raw_sem.at[1, 2])
    far_turned = raw[1].reshape(PIECE, HEAD_DIM).astype(f32).T.astype(bf16)
    for i in (0, 1):

        @pl.when(core == i)
        def _():
            kv[HERE, parity, i, 1, 1 - plane] = far_turned[i * HALF : (i + 1) * HALF]

    for hop in (2, -2, 1, -1):
        send_z(3, 0, hop)
    spread(0, 0, 0, 1)
    own_mask.wait()

    zh = c // RING

    def valid(b):
        return b * RING + x <= r // 2

    side = jnp.where(zl < 2, 3, 1)
    third, fourth = lax.rem(zh + RING - side, RING), lax.rem(zh + 2, RING)
    order = [
        zh,
        lax.rem(zh + side, RING),
        jnp.where(valid(third), third, fourth),
        jnp.where(valid(third), fourth, third),
    ]
    n_late = valid(third).astype(jnp.int32) + valid(fourth).astype(jnp.int32)

    for i in (0, 1):
        last[i] = jnp.int32(NSLOT)
    for place, b in enumerate(order):
        count = jnp.int32(0)
        found_i = [jnp.int32(0)] * SLOTS
        found_j = [jnp.int32(0)] * SLOTS
        for i in (0, 1):
            for j in range(RING):
                flag = mask_ref[2 * r + i, (b * RING + x) * RING + j]
                for s in range(SLOTS):
                    here = flag * jnp.where(count == s, 1, 0)
                    found_i[s] = found_i[s] + here * i
                    found_j[s] = found_j[s] + here * j
                count = count + flag
        for s in range(SLOTS):
            t = place * SLOTS + s
            active = count > s
            i, j = found_i[s], found_j[s]
            info_i[t] = i
            info_j[t] = j
            info_prev[t] = jnp.where(i == 0, last[0], last[1])
            info_diag[t] = jnp.where(2 * r + i == (b * RING + x) * RING + j, 1, 0)
            last[0] = jnp.where(jnp.logical_and(active, i == 0), t, last[0])
            last[1] = jnp.where(jnp.logical_and(active, i == 1), t, last[1])
    key_at = lax.broadcasted_iota(jnp.int32, (BLOCK, BLOCK), 0)
    query_at = lax.broadcasted_iota(jnp.int32, (BLOCK, BLOCK), 1)
    cap[0] = jnp.full((BLOCK, BLOCK), NO_CAP, f32)
    cap[1] = jnp.where(key_at <= query_at, NO_CAP, NEG_FILL)
    for head in range(RING):
        state[head, NSLOT] = jnp.zeros(state.shape[2:], f32)
        maxima[head, NSLOT] = jnp.full(maxima.shape[2:], NEG_FILL, f32)

    ones = jnp.ones((SUMROWS, BLOCK), bf16)

    def late_tile(kind, t, n):
        b = jnp.where(t < 3 * SLOTS, order[2], order[3])
        j = info_j[t]
        return kv[lax.rem(b * RING + n - z + HERE + ZRING, ZRING), lax.rem(j, 2), :, kind, j // 2]

    def near_tile(near):
        def tile(kind, t, n):
            j = info_j[t]
            return near[n, lax.rem(j, 2), :, kind, j // 2]

        return tile

    def score(tile, head, t):
        keys = jnp.concatenate([tile(0, t, n).reshape(PIECE, HEAD_DIM) for n in range(RING)], axis=0)
        return dot(keys, qg[head, info_i[t]], ((1,), (1,)))

    def soften(tile, head, t, s):
        prev = info_prev[t]
        s = jnp.minimum(s, cap[info_diag[t]])
        old_max = maxima[head, prev]
        new_max = jnp.maximum(old_max, jnp.max(s, axis=0, keepdims=True))
        factor = jnp.exp2((old_max - new_max) * EXP_SCALE)
        weights = jnp.exp2((s - new_max) * EXP_SCALE).astype(bf16)
        values = jnp.concatenate([tile(1, t, n).reshape(PIECE, HEAD_DIM) for n in range(RING)], axis=1)
        values = jnp.concatenate([values, ones], axis=0)
        maxima[head, t] = new_max
        state[head, t] = state[head, prev] * factor + dot(values, weights, ((1,), (0,)))

    def stretch(tile, head, t, next_head, next_t):
        for s in range(SLOTS):
            if s < SLOTS - 1:
                scores[s + 1] = score(tile, head, t + s + 1)
            else:
                scores[0] = score(tile, next_head, next_t)
            soften(tile, head, t + s, scores[s])

    def early(near, place, first, count):
        tile, t = near_tile(near), place * SLOTS

        @pl.when(valid(order[place]))
        def _():
            scores[0] = score(tile, first, t)

            def head_body(head, carry):
                stretch(tile, head, t, lax.rem(head + 1, RING), t)
                return carry

            lax.fori_loop(first, first + count, head_body, 0)

    def bring(near, place):
        first = lax.rem(order[place] * RING - z + HERE + ZRING, ZRING)
        return pltpu.make_async_copy(kv.at[pl.ds(first, RING)], near, near_sem.at[place])

    def wait_shared(n):
        for way, first, count in arrivals(n):
            drain(shared(first, count, 1 - core), sib_recv.at[n, way])

    for n in range(1, ROUNDS + 1):
        for hops in ((2, -2), (1, -1)):
            for stream in range(4):
                for hop in hops:
                    o = -2 * n if hop > 0 else 2 * n
                    if n < ROUNDS and abs(hop) == 2:
                        wait_z(stream, o)
                    if n < ROUNDS and o - hop <= LAST:
                        send_z(stream, o, hop)
        for way, first, count in arrivals(n):
            for o in range(first, first + count):
                if n == ROUNDS or abs(o) % 2:
                    for stream in range(4):
                        wait_z(stream, o)
            spread(n, way, first, count)
        for way, first, count in arrivals(n - 1):
            gathered(n - 1, way, first, count)
            share(n - 1, way, first, count)
        if n == ROUNDS - 1:
            own_q.wait()
            for d in (1, 2, 3):
                q_copies[d - 1].wait_recv()
            for m in range(n):
                wait_shared(m)
            copy = bring(near0, 0)
            copy.start()
            copy.wait()
            early(near0, 0, 0, 2)
    early(near0, 0, 2, 2)
    for way, first, count in arrivals(ROUNDS):
        gathered(ROUNDS, way, first, count)
        share(ROUNDS, way, first, count)
    wait_shared(ROUNDS - 1)
    copy = bring(near1, 1)
    copy.start()
    copy.wait()
    early(near1, 1, 0, 4)
    wait_shared(ROUNDS)

    def message(m):
        head, i, to, into = (
            (2, 0, 1, oin.at[0]),
            (2, 1, 3, oin.at[1]),
            (1, 1, 1, orecv.at[0, 1]),
            (3, 0, 3, orecv.at[1, 0]),
            (1, 0, 1, orecv.at[0, 0]),
            (3, 1, 3, orecv.at[1, 1]),
        )[m]
        stats = (sin.at[0], sin.at[1], srecv.at[0, 1], srecv.at[1, 0], srecv.at[0, 0], srecv.at[1, 1])[m]
        return (
            remote(osend.at[head, i], into, o_sem.at[0, m], o_sem.at[1, m], at_x(to)),
            remote(ssend.at[head, i], stats, s_sem.at[0, m], s_sem.at[1, m], at_x(to)),
        )

    def send(*messages):
        for m in messages:
            for copy in message(m):
                copy.start()

    def arrived(*messages):
        for m in messages:
            for copy in message(m):
                copy.wait_recv()

    def merged(parts):
        tops = [stats[0:1] for _, stats in parts]
        top = functools.reduce(jnp.maximum, tops)
        shares = [jnp.exp2((a - top) * EXP_SCALE) for a in tops]
        total = sum(stats[1:2] * a for (_, stats), a in zip(parts, shares))
        return [p.astype(f32) for p, _ in parts], shares, top, total

    def head_of(n):
        return jnp.where(n == 0, 2, jnp.where(n == 1, 1, jnp.where(n == 2, 3, 0)))

    late = 2 * SLOTS
    scores[0] = score(late_tile, head_of(0), late)

    def head_body(n, carry):
        head = head_of(n)

        def stretch_body(place, inner):
            done = place == n_late - 1
            stretch(
                late_tile,
                head,
                late + place * SLOTS,
                jnp.where(done, head_of(n + 1), head),
                jnp.where(done, late, jnp.minimum(late + (place + 1) * SLOTS, NSLOT - 1)),
            )
            return inner

        lax.fori_loop(0, n_late, stretch_body, 0)
        for i in (0, 1):
            final = state[head, last[i]]
            osend[head, i] = final[:HEAD_DIM].astype(bf16)
            ssend[head, i, 0:1] = maxima[head, last[i]]
            ssend[head, i, 1:2] = final[HEAD_DIM : HEAD_DIM + 1]

        @pl.when(n == 0)
        def _():
            send(0, 1)

        @pl.when(n == 1)
        def _():
            send(2)

        @pl.when(n == 2)
        def _():
            send(3)

        return carry

    lax.fori_loop(0, RING, head_body, 0)
    arrived(0, 1)
    for head, i in ((1, 0), (3, 1)):
        parts = [(osend[head, i], ssend[head, i]), (oin[i], sin[i])]
        values, shares, top, total = merged(parts)
        osend[head, i] = sum(p * a for p, a in zip(values, shares)).astype(bf16)
        ssend[head, i, 0:1] = top
        ssend[head, i, 1:2] = total
    send(4, 5)
    arrived(2, 3, 4, 5)
    for i in (0, 1):
        parts = [(osend[0, i], ssend[0, i]), (orecv[0, i], srecv[0, i]), (orecv[1, i], srecv[1, i])]
        values, shares, top, total = merged(parts)
        o_ref[i] = sum(p * (a / total) for p, a in zip(values, shares)).astype(bf16)

    for d in (1, 2, 3):
        q_copies[d - 1].wait_send()
    for m in range(MESSAGES):
        for copy in message(m):
            copy.wait_send()
    for copy in first_copies:
        copy.wait_send()
    drain(kv.at[:, :, core, :, 0], yb_send)
    for stream in range(4):
        drain(kv.at[pl.ds(0, ZRING - 1), parity, core, 0, 0], z_send.at[stream])
    drain(kv.at[:, :, core], sib_send)


def body(queries, key_vectors, value_vectors, block_mask):
    rows, width = queries.shape
    vmem = pl.BlockSpec(memory_space=pltpu.VMEM)
    dma = pltpu.SemaphoreType.DMA
    turned = pl.pallas_call(
        kernel,
        out_shape=jax.ShapeDtypeStruct((2, width, BLOCK), bf16),
        in_specs=[pl.BlockSpec(memory_space=pltpu.HBM)] * 4,
        out_specs=vmem,
        scratch_shapes=[
            pltpu.SMEM(block_mask.shape, jnp.int32),
            pltpu.VMEM((RING, 2, BLOCK, HEAD_DIM), bf16),
            pltpu.VMEM((ZRING, 2, 2, 2, 2, HALF, HEAD_DIM), bf16),
            pltpu.VMEM((2, 2, HALF, HEAD_DIM), bf16),
            pltpu.VMEM((SLOTS, BLOCK, BLOCK), f32),
            pltpu.VMEM((2, BLOCK, BLOCK), f32),
            pltpu.VMEM((RING, 2, 2, 2, 2, HALF, HEAD_DIM), bf16),
            pltpu.VMEM((RING, 2, 2, 2, 2, HALF, HEAD_DIM), bf16),
            pltpu.VMEM((RING, NSLOT + 1, HEAD_DIM + SUMROWS, BLOCK), f32),
            pltpu.VMEM((RING, NSLOT + 1, 1, BLOCK), f32),
            pltpu.VMEM((RING, 2, HEAD_DIM, BLOCK), bf16),
            pltpu.VMEM((2, 2, HEAD_DIM, BLOCK), bf16),
            pltpu.VMEM((2, HEAD_DIM, BLOCK), bf16),
            pltpu.VMEM((RING, 2, 8, BLOCK), f32),
            pltpu.VMEM((2, 2, 8, BLOCK), f32),
            pltpu.VMEM((2, 8, BLOCK), f32),
            pltpu.SMEM((NSLOT,), jnp.int32),
            pltpu.SMEM((NSLOT,), jnp.int32),
            pltpu.SMEM((NSLOT,), jnp.int32),
            pltpu.SMEM((NSLOT,), jnp.int32),
            pltpu.SMEM((2,), jnp.int32),
            dma((4,)),
            dma((2,)),
            dma((2, 3)),
            dma((2,)),
            dma((2, RING)),
            dma,
            dma((ROUNDS + 1, 2, 2)),
            dma((4,)),
            dma((4, ZRING)),
            dma,
            dma((ROUNDS + 1, 2)),
            dma((2, MESSAGES)),
            dma((2, MESSAGES)),
        ],
        compiler_params=pltpu.CompilerParams(
            collective_id=0, has_side_effects=True, vmem_limit_bytes=58 * 2**20
        ),
    )(block_mask, queries.reshape(2, BLOCK, width), key_vectors, value_vectors)
    return turned.transpose(0, 2, 1).reshape(rows, width)


def solution(mesh):
    placed = (P("row", "col"), P(("col", "row"), None), P(("col", "row"), None), P())
    return jax.shard_map(body, mesh=mesh, in_specs=placed, out_specs=P("row", "col"), check_vma=False)
```

```python
import functools

import jax
import jax.numpy as jnp
from jax import lax
from jax.experimental import pallas as pl
from jax.experimental.pallas import tpu as pltpu
from jax.sharding import PartitionSpec as P

HEAD_DIM = 128
BLOCK = 512
SLOTS = 3
RING = 4
ZRING = 16
NSLOT = SLOTS * RING
PIECE = 128
HALF = 64
SUMROWS = 16
HERE = 8
LAST = 7
ROUNDS = 4
MESSAGES = 6
EARLY = 2
NEG_FILL = -1e30
NO_CAP = 3e38
EXP_SCALE = 1.4426950408889634 * HEAD_DIM**-0.5
MESH = pl.DeviceIdType.MESH
f32 = jnp.float32
bf16 = jnp.bfloat16


def dot(a, b, dims):
    return lax.dot_general(a, b, (dims, ((), ())), preferred_element_type=f32)


def kernel(
    mask_hbm,
    q_ref,
    k_ref,
    v_ref,
    o_ref,
    mask_ref,
    qg,
    kv,
    raw,
    scores,
    cap,
    near0,
    near1,
    state,
    maxima,
    osend,
    orecv,
    oin,
    ssend,
    srecv,
    sin,
    info_i,
    info_j,
    info_prev,
    info_diag,
    last,
    own_sem,
    near_sem,
    raw_sem,
    far_sem,
    q_sem,
    yb_send,
    yb_recv,
    z_send,
    z_recv,
    sib_send,
    sib_recv,
    o_sem,
    s_sem,
):
    r = lax.axis_index("row")
    c = lax.axis_index("col")
    core = lax.rem(r, 2)
    zl = lax.rem(r // 2, RING)
    y = r // 8
    x = lax.rem(c, RING)
    z = (c // RING) * RING + zl
    parity, plane = lax.rem(y, 2), y // 2

    def at_x(d):
        return (r, (c // RING) * RING + lax.rem(x + d, RING))

    def at_y(d):
        return (lax.rem(y + d, RING) * 8 + lax.rem(r, 8), c)

    def at_z(d):
        t = lax.rem(z + d + ZRING, ZRING)
        return (y * 8 + lax.rem(t, RING) * 2 + core, (t // RING) * RING + x)

    sibling = (r + 1 - 2 * core, c)
    far = at_y(2)
    far_sibling = (far[0] + 1 - 2 * core, c)

    def remote(src, dst, send, recv, device):
        return pltpu.make_async_remote_copy(
            src_ref=src, dst_ref=dst, send_sem=send, recv_sem=recv, device_id=device, device_id_type=MESH
        )

    def drain(view, sem):
        pltpu.make_async_copy(view, view, sem).wait()

    own_k = pltpu.make_async_copy(k_ref, kv.at[HERE, parity, core, 0, plane], own_sem.at[0])
    own_v = pltpu.make_async_copy(v_ref, raw.at[0, core], own_sem.at[1])
    own_q = pltpu.make_async_copy(q_ref, qg.at[0], own_sem.at[2])
    own_mask = pltpu.make_async_copy(mask_hbm, mask_ref, own_sem.at[3])
    for copy in (own_k, own_v, own_q, own_mask):
        copy.start()

    barrier = pltpu.get_barrier_semaphore()
    partners = [sibling, far_sibling] + [at_z(d) for d in (1, -1, 2, -2)]
    partners += [at_x(d) for d in (1, 2, 3)] + [at_y(d) for d in (1, 2, 3)]
    for partner in partners:
        pl.semaphore_signal(barrier, inc=1, device_id=partner, device_id_type=MESH)
    pl.semaphore_wait(barrier, len(partners))

    first_copies = [
        remote(k_ref, kv.at[HERE, parity, core, 0, plane], far_sem.at[0], far_sem.at[1], far),
        remote(v_ref, raw.at[0, core], raw_sem.at[0, 0], raw_sem.at[1, 0], sibling),
        remote(v_ref, raw.at[1, core], raw_sem.at[0, 1], raw_sem.at[1, 1], far),
        remote(v_ref, raw.at[1, core], raw_sem.at[0, 2], raw_sem.at[1, 2], far_sibling),
    ]
    for copy in first_copies:
        copy.start()
    q_copies = [remote(q_ref, qg.at[RING - d], q_sem.at[0, d], q_sem.at[1, RING - d], at_x(d)) for d in (1, 2, 3)]
    for copy in q_copies:
        copy.start()

    def slab(stream, o):
        return kv.at[HERE + o, parity, core, stream % 2, plane if stream < 2 else 1 - plane]

    def send_z(stream, o, hop, source=None):
        remote(
            slab(stream, o) if source is None else source, slab(stream, o - hop), z_send.at[stream], z_recv.at[stream, HERE + o - hop], at_z(hop)
        ).start()

    def wait_z(stream, o):
        drain(slab(stream, o), z_recv.at[stream, HERE + o])

    def pieces(first, count, from_y):
        return kv.at[pl.ds(HERE + first, count), lax.rem(from_y, 2), core, :, from_y // 2]

    def spread(n, way, first, count):
        for d in (1, 3):
            view = pieces(first, count, y)
            remote(view, view, yb_send, yb_recv.at[n, way, d // 2], at_y(d)).start()

    def gathered(n, way, first, count):
        for d in (1, 3):
            drain(pieces(first, count, lax.rem(y + RING - d, RING)), yb_recv.at[n, way, d // 2])

    def shared(first, count, of_core):
        return kv.at[pl.ds(HERE + first, count), :, of_core]

    def share(n, way, first, count):
        view = shared(first, count, core)
        remote(view, view, sib_send, sib_recv.at[n, way], sibling).start()

    def arrivals(n):
        if n == 0:
            return [(0, 0, 1)]
        return [(0, -2 * n, 2), (1, 2 * n - 1, 2 if n < ROUNDS else 1)]

    for hop in (2, -2, 1, -1):
        send_z(0, 0, hop, k_ref)
    own_k.wait()
    own_v.wait()
    drain(raw.at[0, 1 - core], raw_sem.at[1, 0])
    own_turned = raw[0].reshape(PIECE, HEAD_DIM).astype(f32).T.astype(bf16)
    for i in (0, 1):

        @pl.when(core == i)
        def _():
            kv[HERE, parity, i, 1, plane] = own_turned[i * HALF : (i + 1) * HALF]

    for hop in (2, -2, 1, -1):
        send_z(1, 0, hop)
    drain(kv.at[HERE, parity, core, 0, 1 - plane], far_sem.at[1])
    for hop in (2, -2, 1, -1):
        send_z(2, 0, hop)
    drain(raw.at[1, core], raw_sem.at[1, 1])
    drain(raw.at[1, 1 - core], raw_sem.at[1, 2])
    far_turned = raw[1].reshape(PIECE, HEAD_DIM).astype(f32).T.astype(bf16)
    for i in (0, 1):

        @pl.when(core == i)
        def _():
            kv[HERE, parity, i, 1, 1 - plane] = far_turned[i * HALF : (i + 1) * HALF]

    for hop in (2, -2, 1, -1):
        send_z(3, 0, hop)
    spread(0, 0, 0, 1)

    zh = c // RING

    def valid(b):
        return b * RING + x <= r // 2

    def on_diagonal(b):
        return b * RING + x == r // 2

    side = jnp.where(zl < 2, 3, 1)
    third, fourth = lax.rem(zh + RING - side, RING), lax.rem(zh + 2, RING)
    order = [
        zh,
        lax.rem(zh + side, RING),
        jnp.where(valid(third), third, fourth),
        jnp.where(valid(third), fourth, third),
    ]
    n_late = valid(third).astype(jnp.int32) + valid(fourth).astype(jnp.int32)

    def prepare():
        for i in (0, 1):
            last[i] = jnp.int32(NSLOT)
        for place, b in enumerate(order):
            count = jnp.int32(0)
            found_i = [jnp.int32(0)] * SLOTS
            found_j = [jnp.int32(0)] * SLOTS
            for i in (0, 1):
                for j in range(RING):
                    flag = mask_ref[2 * r + i, (b * RING + x) * RING + j]
                    for s in range(SLOTS):
                        here = flag * jnp.where(count == s, 1, 0)
                        found_i[s] = found_i[s] + here * i
                        found_j[s] = found_j[s] + here * j
                    count = count + flag
            for s in range(SLOTS):
                t = place * SLOTS + s
                active = count > s
                i, j = found_i[s], found_j[s]
                info_i[t] = i
                info_j[t] = j
                info_prev[t] = jnp.where(i == 0, last[0], last[1])
                info_diag[t] = jnp.where(2 * r + i == (b * RING + x) * RING + j, 1, 0)
                last[0] = jnp.where(jnp.logical_and(active, i == 0), t, last[0])
                last[1] = jnp.where(jnp.logical_and(active, i == 1), t, last[1])
        key_at = lax.broadcasted_iota(jnp.int32, (BLOCK, BLOCK), 0)
        query_at = lax.broadcasted_iota(jnp.int32, (BLOCK, BLOCK), 1)
        cap[0] = jnp.full((BLOCK, BLOCK), NO_CAP, f32)
        cap[1] = jnp.where(key_at <= query_at, NO_CAP, NEG_FILL)
        for head in range(RING):
            state[head, NSLOT] = jnp.zeros(state.shape[2:], f32)
            maxima[head, NSLOT] = jnp.full(maxima.shape[2:], NEG_FILL, f32)

    ones = jnp.ones((SUMROWS, BLOCK), bf16)

    def at_place(place):
        return jnp.where(place == 1, order[1], jnp.where(place == 2, order[2], order[3]))

    def late_tile(kind, t, n):
        b = at_place(t // SLOTS)
        j = info_j[t]
        return kv[lax.rem(b * RING + n - z + HERE + ZRING, ZRING), lax.rem(j, 2), :, kind, j // 2]

    def near_tile(near):
        def tile(kind, t, n):
            j = info_j[t]
            return near[n, lax.rem(j, 2), :, kind, j // 2]

        return tile

    def score(tile, head, t):
        keys = jnp.concatenate([tile(0, t, n).reshape(PIECE, HEAD_DIM) for n in range(RING)], axis=0)
        return dot(keys, qg[head, info_i[t]], ((1,), (1,)))

    def soften(tile, head, t, s, masked):
        prev = info_prev[t]
        if masked:
            s = jnp.minimum(s, cap[info_diag[t]])
        old_max = maxima[head, prev]
        new_max = jnp.maximum(old_max, jnp.max(s, axis=0, keepdims=True))
        factor = jnp.exp2((old_max - new_max) * EXP_SCALE)
        weights = jnp.exp2((s - new_max) * EXP_SCALE).astype(bf16)
        values = jnp.concatenate([tile(1, t, n).reshape(PIECE, HEAD_DIM) for n in range(RING)], axis=1)
        values = jnp.concatenate([values, ones], axis=0)
        maxima[head, t] = new_max
        state[head, t] = state[head, prev] * factor + dot(values, weights, ((1,), (0,)))

    def stretch(tile, head, t, next_head, next_t, masked):
        for s in range(SLOTS):
            if s < SLOTS - 1:
                scores[s + 1] = score(tile, head, t + s + 1)
            else:
                scores[0] = score(tile, next_head, next_t)
            soften(tile, head, t + s, scores[s], masked)

    def head_of(n):
        return jnp.where(n == 0, 2, jnp.where(n == 1, 1, jnp.where(n == 2, 3, 0)))

    def early(near, place, count):
        tile, t = near_tile(near), place * SLOTS

        def heads(masked):
            scores[0] = score(tile, head_of(0), t)

            def head_body(n, carry):
                stretch(tile, head_of(n), t, head_of(n + 1), t, masked)
                return carry

            lax.fori_loop(0, count, head_body, 0)

        on = on_diagonal(order[place])
        pl.when(jnp.logical_and(valid(order[place]), jnp.logical_not(on)))(lambda: heads(False))
        pl.when(jnp.logical_and(valid(order[place]), on))(lambda: heads(True))

    def bring(near, place):
        first = lax.rem(order[place] * RING - z + HERE + ZRING, ZRING)
        return pltpu.make_async_copy(kv.at[pl.ds(first, RING)], near, near_sem.at[place])

    def wait_shared(n):
        for way, first, count in arrivals(n):
            drain(shared(first, count, 1 - core), sib_recv.at[n, way])

    for n in range(1, ROUNDS + 1):
        for hops in ((2, -2), (1, -1)):
            for stream in range(4):
                for hop in hops:
                    o = -2 * n if hop > 0 else 2 * n
                    if n < ROUNDS and abs(hop) == 2:
                        wait_z(stream, o)
                    if n < ROUNDS and o - hop <= LAST:
                        send_z(stream, o, hop)
        for way, first, count in arrivals(n):
            for o in range(first, first + count):
                if n == ROUNDS or abs(o) % 2:
                    for stream in range(4):
                        wait_z(stream, o)
            spread(n, way, first, count)
        for way, first, count in arrivals(n - 1):
            gathered(n - 1, way, first, count)
            share(n - 1, way, first, count)
        if n == 1:
            own_mask.wait()
            prepare()
        if n == ROUNDS - 1:
            own_q.wait()
            for d in (1, 2, 3):
                q_copies[d - 1].wait_recv()
            for m in range(n):
                wait_shared(m)
            copy = bring(near0, 0)
            copy.start()
            copy.wait()
    early(near0, 0, RING)
    for way, first, count in arrivals(ROUNDS):
        gathered(ROUNDS, way, first, count)
        share(ROUNDS, way, first, count)
    wait_shared(ROUNDS - 1)
    copy = bring(near1, 1)
    copy.start()
    copy.wait()
    early(near1, 1, EARLY)
    wait_shared(ROUNDS)

    def message(m):
        head, i, to, into = (
            (2, 0, 1, oin.at[0]),
            (2, 1, 3, oin.at[1]),
            (1, 1, 1, orecv.at[0, 1]),
            (3, 0, 3, orecv.at[1, 0]),
            (1, 0, 1, orecv.at[0, 0]),
            (3, 1, 3, orecv.at[1, 1]),
        )[m]
        stats = (sin.at[0], sin.at[1], srecv.at[0, 1], srecv.at[1, 0], srecv.at[0, 0], srecv.at[1, 1])[m]
        return (
            remote(osend.at[head, i], into, o_sem.at[0, m], o_sem.at[1, m], at_x(to)),
            remote(ssend.at[head, i], stats, s_sem.at[0, m], s_sem.at[1, m], at_x(to)),
        )

    def send(*messages):
        for m in messages:
            for copy in message(m):
                copy.start()

    def arrived(*messages):
        for m in messages:
            for copy in message(m):
                copy.wait_recv()

    def merged(parts):
        tops = [stats[0:1] for _, stats in parts]
        top = functools.reduce(jnp.maximum, tops)
        shares = [jnp.exp2((a - top) * EXP_SCALE) for a in tops]
        total = sum(stats[1:2] * a for (_, stats), a in zip(parts, shares))
        return [p.astype(f32) for p, _ in parts], shares, top, total

    def first_of(n):
        return jnp.where(jnp.logical_and(n >= EARLY, valid(order[1])), 1, 2)

    scores[0] = score(late_tile, head_of(0), first_of(0) * SLOTS)

    def head_body(n, carry):
        head = head_of(n)

        @pl.when(n_late == 0)
        def _():
            scores[0] = score(late_tile, head, first_of(n) * SLOTS)

        def stretch_body(place, inner):
            done = place == n_late + 1
            slots = (
                late_tile,
                head,
                place * SLOTS,
                jnp.where(done, head_of(n + 1), head),
                jnp.where(done, first_of(n + 1), jnp.minimum(place + 1, RING - 1)) * SLOTS,
            )
            on = on_diagonal(at_place(place))
            pl.when(jnp.logical_not(on))(lambda: stretch(*slots, False))
            pl.when(on)(lambda: stretch(*slots, True))
            return inner

        lax.fori_loop(first_of(n), n_late + 2, stretch_body, 0)
        for i in (0, 1):
            final = state[head, last[i]]
            osend[head, i] = final[:HEAD_DIM].astype(bf16)
            ssend[head, i, 0:1] = maxima[head, last[i]]
            ssend[head, i, 1:2] = final[HEAD_DIM : HEAD_DIM + 1]

        @pl.when(n == 0)
        def _():
            send(0, 1)

        @pl.when(n == 1)
        def _():
            send(2)

        @pl.when(n == 2)
        def _():
            send(3)
            arrived(0, 1)
            for m, other, i in ((4, 1, 0), (5, 3, 1)):
                parts = [(osend[other, i], ssend[other, i]), (oin[i], sin[i])]
                values, shares, top, total = merged(parts)
                osend[other, i] = sum(p * a for p, a in zip(values, shares)).astype(bf16)
                ssend[other, i, 0:1] = top
                ssend[other, i, 1:2] = total
                send(m)

        return carry

    lax.fori_loop(0, RING, head_body, 0)
    arrived(2, 3, 4, 5)
    for i in (0, 1):
        parts = [(osend[0, i], ssend[0, i]), (orecv[0, i], srecv[0, i]), (orecv[1, i], srecv[1, i])]
        values, shares, top, total = merged(parts)
        o_ref[i] = sum(p * (a / total) for p, a in zip(values, shares)).astype(bf16)

    for d in (1, 2, 3):
        q_copies[d - 1].wait_send()
    for m in range(MESSAGES):
        for copy in message(m):
            copy.wait_send()
    for copy in first_copies:
        copy.wait_send()
    drain(kv.at[:, :, core, :, 0], yb_send)
    for stream in range(4):
        drain(kv.at[pl.ds(0, ZRING - 1), parity, core, 0, 0], z_send.at[stream])
    drain(kv.at[:, :, core], sib_send)


def body(queries, key_vectors, value_vectors, block_mask):
    rows, width = queries.shape
    vmem = pl.BlockSpec(memory_space=pltpu.VMEM)
    dma = pltpu.SemaphoreType.DMA
    turned = pl.pallas_call(
        kernel,
        out_shape=jax.ShapeDtypeStruct((2, width, BLOCK), bf16),
        in_specs=[pl.BlockSpec(memory_space=pltpu.HBM)] * 4,
        out_specs=vmem,
        scratch_shapes=[
            pltpu.SMEM(block_mask.shape, jnp.int32),
            pltpu.VMEM((RING, 2, BLOCK, HEAD_DIM), bf16),
            pltpu.VMEM((ZRING, 2, 2, 2, 2, HALF, HEAD_DIM), bf16),
            pltpu.VMEM((2, 2, HALF, HEAD_DIM), bf16),
            pltpu.VMEM((SLOTS, BLOCK, BLOCK), f32),
            pltpu.VMEM((2, BLOCK, BLOCK), f32),
            pltpu.VMEM((RING, 2, 2, 2, 2, HALF, HEAD_DIM), bf16),
            pltpu.VMEM((RING, 2, 2, 2, 2, HALF, HEAD_DIM), bf16),
            pltpu.VMEM((RING, NSLOT + 1, HEAD_DIM + SUMROWS, BLOCK), f32),
            pltpu.VMEM((RING, NSLOT + 1, 1, BLOCK), f32),
            pltpu.VMEM((RING, 2, HEAD_DIM, BLOCK), bf16),
            pltpu.VMEM((2, 2, HEAD_DIM, BLOCK), bf16),
            pltpu.VMEM((2, HEAD_DIM, BLOCK), bf16),
            pltpu.VMEM((RING, 2, 8, BLOCK), f32),
            pltpu.VMEM((2, 2, 8, BLOCK), f32),
            pltpu.VMEM((2, 8, BLOCK), f32),
            pltpu.SMEM((NSLOT,), jnp.int32),
            pltpu.SMEM((NSLOT,), jnp.int32),
            pltpu.SMEM((NSLOT,), jnp.int32),
            pltpu.SMEM((NSLOT,), jnp.int32),
            pltpu.SMEM((2,), jnp.int32),
            dma((4,)),
            dma((2,)),
            dma((2, 3)),
            dma((2,)),
            dma((2, RING)),
            dma,
            dma((ROUNDS + 1, 2, 2)),
            dma((4,)),
            dma((4, ZRING)),
            dma,
            dma((ROUNDS + 1, 2)),
            dma((2, MESSAGES)),
            dma((2, MESSAGES)),
        ],
        compiler_params=pltpu.CompilerParams(
            collective_id=0, has_side_effects=True, vmem_limit_bytes=58 * 2**20
        ),
    )(block_mask, queries.reshape(2, BLOCK, width), key_vectors, value_vectors)
    return turned.transpose(0, 2, 1).reshape(rows, width)


def solution(mesh):
    placed = (P("row", "col"), P(("col", "row"), None), P(("col", "row"), None), P())
    return jax.shard_map(body, mesh=mesh, in_specs=placed, out_specs=P("row", "col"), check_vma=False)
```

```python
import functools

import jax
import jax.numpy as jnp
from jax import lax
from jax.experimental import pallas as pl
from jax.experimental.pallas import tpu as pltpu
from jax.sharding import PartitionSpec as P

HEAD_DIM = 128
BLOCK = 512
SLOTS = 3
RING = 4
ZRING = 16
NSLOT = SLOTS * RING
PIECE = 128
HALF = 64
SUMROWS = 16
HERE = 8
LAST = 7
ROUNDS = 4
MESSAGES = 6
EARLY = 3
NEG_FILL = -1e30
NO_CAP = 3e38
EXP_SCALE = 1.4426950408889634 * HEAD_DIM**-0.5
MESH = pl.DeviceIdType.MESH
f32 = jnp.float32
bf16 = jnp.bfloat16


def dot(a, b, dims):
    return lax.dot_general(a, b, (dims, ((), ())), preferred_element_type=f32)


def kernel(
    mask_hbm,
    q_ref,
    k_ref,
    v_ref,
    o_ref,
    mask_ref,
    qg,
    kv,
    raw,
    scores,
    cap,
    near0,
    near1,
    state,
    maxima,
    osend,
    orecv,
    oin,
    ssend,
    srecv,
    sin,
    obuf,
    info_i,
    info_j,
    info_prev,
    info_diag,
    last,
    own_sem,
    near_sem,
    raw_sem,
    far_sem,
    q_sem,
    yb_send,
    yb_recv,
    z_send,
    z_recv,
    sib_send,
    sib_recv,
    o_sem,
    s_sem,
    out_sem,
):
    r = lax.axis_index("row")
    c = lax.axis_index("col")
    core = lax.rem(r, 2)
    zl = lax.rem(r // 2, RING)
    y = r // 8
    x = lax.rem(c, RING)
    z = (c // RING) * RING + zl
    parity, plane = lax.rem(y, 2), y // 2

    def at_x(d):
        return (r, (c // RING) * RING + lax.rem(x + d, RING))

    def at_y(d):
        return (lax.rem(y + d, RING) * 8 + lax.rem(r, 8), c)

    def at_z(d):
        t = lax.rem(z + d + ZRING, ZRING)
        return (y * 8 + lax.rem(t, RING) * 2 + core, (t // RING) * RING + x)

    sibling = (r + 1 - 2 * core, c)
    far = at_y(2)
    far_sibling = (far[0] + 1 - 2 * core, c)

    def remote(src, dst, send, recv, device):
        return pltpu.make_async_remote_copy(
            src_ref=src, dst_ref=dst, send_sem=send, recv_sem=recv, device_id=device, device_id_type=MESH
        )

    def drain(view, sem):
        pltpu.make_async_copy(view, view, sem).wait()

    own_k = pltpu.make_async_copy(k_ref, kv.at[HERE, parity, core, 0, plane], own_sem.at[0])
    own_v = pltpu.make_async_copy(v_ref, raw.at[0, core], own_sem.at[1])
    own_q = pltpu.make_async_copy(q_ref, qg.at[0], own_sem.at[2])
    own_mask = pltpu.make_async_copy(mask_hbm, mask_ref, own_sem.at[3])
    for copy in (own_k, own_v, own_q, own_mask):
        copy.start()

    barrier = pltpu.get_barrier_semaphore()
    partners = [sibling, far_sibling] + [at_z(d) for d in (1, -1, 2, -2)]
    partners += [at_x(d) for d in (1, 2, 3)] + [at_y(d) for d in (1, 2, 3)]
    for partner in partners:
        pl.semaphore_signal(barrier, inc=1, device_id=partner, device_id_type=MESH)
    pl.semaphore_wait(barrier, len(partners))

    first_copies = [
        remote(k_ref, kv.at[HERE, parity, core, 0, plane], far_sem.at[0], far_sem.at[1], far),
        remote(v_ref, raw.at[0, core], raw_sem.at[0, 0], raw_sem.at[1, 0], sibling),
        remote(v_ref, raw.at[1, core], raw_sem.at[0, 1], raw_sem.at[1, 1], far),
        remote(v_ref, raw.at[1, core], raw_sem.at[0, 2], raw_sem.at[1, 2], far_sibling),
    ]
    for copy in first_copies:
        copy.start()
    q_copies = [remote(q_ref, qg.at[RING - d], q_sem.at[0, d], q_sem.at[1, RING - d], at_x(d)) for d in (1, 2, 3)]
    for copy in q_copies:
        copy.start()

    def slab(stream, o):
        return kv.at[HERE + o, parity, core, stream % 2, plane if stream < 2 else 1 - plane]

    def send_z(stream, o, hop, source=None):
        remote(
            slab(stream, o) if source is None else source, slab(stream, o - hop), z_send.at[stream], z_recv.at[stream, HERE + o - hop], at_z(hop)
        ).start()

    def wait_z(stream, o):
        drain(slab(stream, o), z_recv.at[stream, HERE + o])

    def pieces(first, count, from_y):
        return kv.at[pl.ds(HERE + first, count), lax.rem(from_y, 2), core, :, from_y // 2]

    def spread(n, way, first, count):
        for d in (1, 3):
            view = pieces(first, count, y)
            remote(view, view, yb_send, yb_recv.at[n, way, d // 2], at_y(d)).start()

    def gathered(n, way, first, count):
        for d in (1, 3):
            drain(pieces(first, count, lax.rem(y + RING - d, RING)), yb_recv.at[n, way, d // 2])

    def shared(first, count, of_core, of_parity):
        return kv.at[pl.ds(HERE + first, count), of_parity, of_core]

    def share(n, way, first, count, part):
        view = shared(first, count, core, parity if part == 0 else 1 - parity)
        remote(view, view, sib_send, sib_recv.at[n, way, part], sibling).start()

    def arrivals(n):
        if n == 0:
            return [(0, 0, 1)]
        return [(0, -2 * n, 2), (1, 2 * n - 1, 2 if n < ROUNDS else 1)]

    for hop in (2, -2, 1, -1):
        send_z(0, 0, hop, k_ref)
    own_k.wait()
    own_v.wait()
    drain(raw.at[0, 1 - core], raw_sem.at[1, 0])
    own_turned = raw[0].reshape(PIECE, HEAD_DIM).astype(f32).T.astype(bf16)
    for i in (0, 1):

        @pl.when(core == i)
        def _():
            kv[HERE, parity, i, 1, plane] = own_turned[i * HALF : (i + 1) * HALF]

    for hop in (2, -2, 1, -1):
        send_z(1, 0, hop)
    drain(kv.at[HERE, parity, core, 0, 1 - plane], far_sem.at[1])
    for hop in (2, -2, 1, -1):
        send_z(2, 0, hop)
    drain(raw.at[1, core], raw_sem.at[1, 1])
    drain(raw.at[1, 1 - core], raw_sem.at[1, 2])
    far_turned = raw[1].reshape(PIECE, HEAD_DIM).astype(f32).T.astype(bf16)
    for i in (0, 1):

        @pl.when(core == i)
        def _():
            kv[HERE, parity, i, 1, 1 - plane] = far_turned[i * HALF : (i + 1) * HALF]

    for hop in (2, -2, 1, -1):
        send_z(3, 0, hop)
    spread(0, 0, 0, 1)
    share(0, 0, 0, 1, 0)

    zh = c // RING

    def valid(b):
        return b * RING + x <= r // 2

    def on_diagonal(b):
        return b * RING + x == r // 2

    side = jnp.where(zl < 2, 3, 1)
    third, fourth = lax.rem(zh + RING - side, RING), lax.rem(zh + 2, RING)
    order = [
        zh,
        lax.rem(zh + side, RING),
        jnp.where(valid(third), third, fourth),
        jnp.where(valid(third), fourth, third),
    ]
    n_late = valid(third).astype(jnp.int32) + valid(fourth).astype(jnp.int32)

    def prepare():
        for i in (0, 1):
            last[i] = jnp.int32(NSLOT)
        for place, b in enumerate(order):
            count = jnp.int32(0)
            found_i = [jnp.int32(0)] * SLOTS
            found_j = [jnp.int32(0)] * SLOTS
            for i in (0, 1):
                for j in range(RING):
                    flag = mask_ref[2 * r + i, (b * RING + x) * RING + j]
                    for s in range(SLOTS):
                        here = flag * jnp.where(count == s, 1, 0)
                        found_i[s] = found_i[s] + here * i
                        found_j[s] = found_j[s] + here * j
                    count = count + flag
            for s in range(SLOTS):
                t = place * SLOTS + s
                active = count > s
                i, j = found_i[s], found_j[s]
                info_i[t] = i
                info_j[t] = j
                info_prev[t] = jnp.where(i == 0, last[0], last[1])
                info_diag[t] = jnp.where(2 * r + i == (b * RING + x) * RING + j, 1, 0)
                last[0] = jnp.where(jnp.logical_and(active, i == 0), t, last[0])
                last[1] = jnp.where(jnp.logical_and(active, i == 1), t, last[1])
        key_at = lax.broadcasted_iota(jnp.int32, (BLOCK, BLOCK), 0)
        query_at = lax.broadcasted_iota(jnp.int32, (BLOCK, BLOCK), 1)
        cap[0] = jnp.full((BLOCK, BLOCK), NO_CAP, f32)
        cap[1] = jnp.where(key_at <= query_at, NO_CAP, NEG_FILL)
        for head in range(RING):
            state[head, NSLOT] = jnp.zeros(state.shape[2:], f32)
            maxima[head, NSLOT] = jnp.full(maxima.shape[2:], NEG_FILL, f32)

    ones = jnp.ones((SUMROWS, BLOCK), bf16)

    def at_place(place):
        return jnp.where(place == 1, order[1], jnp.where(place == 2, order[2], order[3]))

    def late_tile(kind, t, n):
        b = at_place(t // SLOTS)
        j = info_j[t]
        return kv[lax.rem(b * RING + n - z + HERE + ZRING, ZRING), lax.rem(j, 2), :, kind, j // 2]

    def near_tile(near):
        def tile(kind, t, n):
            j = info_j[t]
            return near[n, lax.rem(j, 2), :, kind, j // 2]

        return tile

    def score(tile, head, t):
        keys = jnp.concatenate([tile(0, t, n).reshape(PIECE, HEAD_DIM) for n in range(RING)], axis=0)
        return dot(keys, qg[head, info_i[t]], ((1,), (1,)))

    def soften(tile, head, t, s, masked):
        prev = info_prev[t]
        if masked:
            s = jnp.minimum(s, cap[info_diag[t]])
        old_max = maxima[head, prev]
        new_max = jnp.maximum(old_max, jnp.max(s, axis=0, keepdims=True))
        factor = jnp.exp2((old_max - new_max) * EXP_SCALE)
        weights = jnp.exp2((s - new_max) * EXP_SCALE).astype(bf16)
        values = jnp.concatenate([tile(1, t, n).reshape(PIECE, HEAD_DIM) for n in range(RING)], axis=1)
        values = jnp.concatenate([values, ones], axis=0)
        maxima[head, t] = new_max
        state[head, t] = state[head, prev] * factor + dot(values, weights, ((1,), (0,)))

    def stretch(tile, head, t, next_head, next_t, masked):
        for s in range(SLOTS):
            if s < SLOTS - 1:
                scores[s + 1] = score(tile, head, t + s + 1)
            else:
                scores[0] = score(tile, next_head, next_t)
            soften(tile, head, t + s, scores[s], masked)

    def head_of(n):
        return jnp.where(n == 0, 2, jnp.where(n == 1, 1, jnp.where(n == 2, 3, 0)))

    def early(near, place, count):
        tile, t = near_tile(near), place * SLOTS

        def heads(masked):
            scores[0] = score(tile, head_of(0), t)

            def head_body(n, carry):
                stretch(tile, head_of(n), t, head_of(n + 1), t, masked)
                return carry

            lax.fori_loop(0, count, head_body, 0)

        on = on_diagonal(order[place])
        pl.when(jnp.logical_and(valid(order[place]), jnp.logical_not(on)))(lambda: heads(False))
        pl.when(jnp.logical_and(valid(order[place]), on))(lambda: heads(True))

    def bring(near, place):
        first = lax.rem(order[place] * RING - z + HERE + ZRING, ZRING)
        return pltpu.make_async_copy(kv.at[pl.ds(first, RING)], near, near_sem.at[place])

    def wait_shared(n):
        for way, first, count in arrivals(n):
            drain(shared(first, count, 1 - core, parity), sib_recv.at[n, way, 0])
            drain(shared(first, count, 1 - core, 1 - parity), sib_recv.at[n, way, 1])

    for n in range(1, ROUNDS + 1):
        for hops in ((2, -2), (1, -1)):
            for stream in range(4):
                for hop in hops:
                    o = -2 * n if hop > 0 else 2 * n
                    if n < ROUNDS and abs(hop) == 2:
                        wait_z(stream, o)
                    if n < ROUNDS and o - hop <= LAST:
                        send_z(stream, o, hop)
        for way, first, count in arrivals(n):
            for o in range(first, first + count):
                if n == ROUNDS or abs(o) % 2:
                    for stream in range(4):
                        wait_z(stream, o)
            spread(n, way, first, count)
            share(n, way, first, count, 0)
        for way, first, count in arrivals(n - 1):
            gathered(n - 1, way, first, count)
            share(n - 1, way, first, count, 1)
        if n == 1:
            own_mask.wait()
            prepare()
        if n == ROUNDS - 1:
            own_q.wait()
            for d in (1, 2, 3):
                q_copies[d - 1].wait_recv()
            for m in range(n):
                wait_shared(m)
            copy = bring(near0, 0)
            copy.start()
            copy.wait()
    early(near0, 0, RING)
    for way, first, count in arrivals(ROUNDS):
        gathered(ROUNDS, way, first, count)
        share(ROUNDS, way, first, count, 1)
    wait_shared(ROUNDS - 1)
    copy = bring(near1, 1)
    copy.start()
    copy.wait()
    early(near1, 1, EARLY)
    wait_shared(ROUNDS)

    def message(m):
        head, i, to, into = (
            (2, 0, 1, oin.at[0]),
            (2, 1, 3, oin.at[1]),
            (1, 1, 1, orecv.at[0, 1]),
            (3, 0, 3, orecv.at[1, 0]),
            (1, 0, 1, orecv.at[0, 0]),
            (3, 1, 3, orecv.at[1, 1]),
        )[m]
        stats = (sin.at[0], sin.at[1], srecv.at[0, 1], srecv.at[1, 0], srecv.at[0, 0], srecv.at[1, 1])[m]
        return (
            remote(osend.at[head, i], into, o_sem.at[0, m], o_sem.at[1, m], at_x(to)),
            remote(ssend.at[head, i], stats, s_sem.at[0, m], s_sem.at[1, m], at_x(to)),
        )

    def send(*messages):
        for m in messages:
            for copy in message(m):
                copy.start()

    def arrived(*messages):
        for m in messages:
            for copy in message(m):
                copy.wait_recv()

    def merged(parts):
        tops = [stats[0:1] for _, stats in parts]
        top = functools.reduce(jnp.maximum, tops)
        shares = [jnp.exp2((a - top) * EXP_SCALE) for a in tops]
        total = sum(stats[1:2] * a for (_, stats), a in zip(parts, shares))
        return [p.astype(f32) for p, _ in parts], shares, top, total

    def first_of(n):
        return jnp.where(jnp.logical_and(n >= EARLY, valid(order[1])), 1, 2)

    scores[0] = score(late_tile, head_of(0), first_of(0) * SLOTS)

    def head_body(n, carry):
        head = head_of(n)

        @pl.when(n_late == 0)
        def _():
            scores[0] = score(late_tile, head, first_of(n) * SLOTS)

        def stretch_body(place, inner):
            done = place == n_late + 1
            slots = (
                late_tile,
                head,
                place * SLOTS,
                jnp.where(done, head_of(n + 1), head),
                jnp.where(done, first_of(n + 1), jnp.minimum(place + 1, RING - 1)) * SLOTS,
            )
            on = on_diagonal(at_place(place))
            pl.when(jnp.logical_not(on))(lambda: stretch(*slots, False))
            pl.when(on)(lambda: stretch(*slots, True))
            return inner

        lax.fori_loop(first_of(n), n_late + 2, stretch_body, 0)
        for i in (0, 1):
            final = state[head, last[i]]
            osend[head, i] = final[:HEAD_DIM].astype(bf16)
            ssend[head, i, 0:1] = maxima[head, last[i]]
            ssend[head, i, 1:2] = final[HEAD_DIM : HEAD_DIM + 1]

        @pl.when(n == 0)
        def _():
            send(0, 1)

        @pl.when(n == 1)
        def _():
            send(2)

        @pl.when(n == 2)
        def _():
            send(3)
            arrived(0, 1)
            for m, other, i in ((4, 1, 0), (5, 3, 1)):
                parts = [(osend[other, i], ssend[other, i]), (oin[i], sin[i])]
                values, shares, top, total = merged(parts)
                osend[other, i] = sum(p * a for p, a in zip(values, shares)).astype(bf16)
                ssend[other, i, 0:1] = top
                ssend[other, i, 1:2] = total
                send(m)

        return carry

    lax.fori_loop(0, RING, head_body, 0)
    outs = []
    for m, i in ((3, 0), (2, 1)):
        arrived(m)
        parts = [(osend[0, i], ssend[0, i]), (orecv[1 - i, i], srecv[1 - i, i])]
        values, shares, top, total = merged(parts)
        state[0, i, :HEAD_DIM] = sum(p * a for p, a in zip(values, shares))
        state[0, i, HEAD_DIM : HEAD_DIM + 1] = total
        maxima[0, i] = top
    for m, i in ((4, 0), (5, 1)):
        arrived(m)
        tops = [maxima[0, i], srecv[i, i, 0:1]]
        top = jnp.maximum(*tops)
        shares = [jnp.exp2((a - top) * EXP_SCALE) for a in tops]
        total = state[0, i, HEAD_DIM : HEAD_DIM + 1] * shares[0] + srecv[i, i, 1:2] * shares[1]
        shares = [a / total for a in shares]
        obuf[i] = (state[0, i, :HEAD_DIM] * shares[0] + orecv[i, i].astype(f32) * shares[1]).astype(bf16)
        outs.append(pltpu.make_async_copy(obuf.at[i], o_ref.at[i], out_sem.at[i]))
        outs[i].start()

    for d in (1, 2, 3):
        q_copies[d - 1].wait_send()
    for m in range(MESSAGES):
        for copy in message(m):
            copy.wait_send()
    for copy in first_copies:
        copy.wait_send()
    drain(kv.at[:, :, core, :, 0], yb_send)
    for stream in range(4):
        drain(kv.at[pl.ds(0, ZRING - 1), parity, core, 0, 0], z_send.at[stream])
    drain(kv.at[:, :, core], sib_send)
    for copy in outs:
        copy.wait()


def body(queries, key_vectors, value_vectors, block_mask):
    rows, width = queries.shape
    dma = pltpu.SemaphoreType.DMA
    turned = pl.pallas_call(
        kernel,
        out_shape=jax.ShapeDtypeStruct((2, width, BLOCK), bf16),
        in_specs=[pl.BlockSpec(memory_space=pltpu.HBM)] * 4,
        out_specs=pl.BlockSpec(memory_space=pltpu.HBM),
        scratch_shapes=[
            pltpu.SMEM(block_mask.shape, jnp.int32),
            pltpu.VMEM((RING, 2, BLOCK, HEAD_DIM), bf16),
            pltpu.VMEM((ZRING, 2, 2, 2, 2, HALF, HEAD_DIM), bf16),
            pltpu.VMEM((2, 2, HALF, HEAD_DIM), bf16),
            pltpu.VMEM((SLOTS, BLOCK, BLOCK), f32),
            pltpu.VMEM((2, BLOCK, BLOCK), f32),
            pltpu.VMEM((RING, 2, 2, 2, 2, HALF, HEAD_DIM), bf16),
            pltpu.VMEM((RING, 2, 2, 2, 2, HALF, HEAD_DIM), bf16),
            pltpu.VMEM((RING, NSLOT + 1, HEAD_DIM + SUMROWS, BLOCK), f32),
            pltpu.VMEM((RING, NSLOT + 1, 1, BLOCK), f32),
            pltpu.VMEM((RING, 2, HEAD_DIM, BLOCK), bf16),
            pltpu.VMEM((2, 2, HEAD_DIM, BLOCK), bf16),
            pltpu.VMEM((2, HEAD_DIM, BLOCK), bf16),
            pltpu.VMEM((RING, 2, 8, BLOCK), f32),
            pltpu.VMEM((2, 2, 8, BLOCK), f32),
            pltpu.VMEM((2, 8, BLOCK), f32),
            pltpu.VMEM((2, HEAD_DIM, BLOCK), bf16),
            pltpu.SMEM((NSLOT,), jnp.int32),
            pltpu.SMEM((NSLOT,), jnp.int32),
            pltpu.SMEM((NSLOT,), jnp.int32),
            pltpu.SMEM((NSLOT,), jnp.int32),
            pltpu.SMEM((2,), jnp.int32),
            dma((4,)),
            dma((2,)),
            dma((2, 3)),
            dma((2,)),
            dma((2, RING)),
            dma,
            dma((ROUNDS + 1, 2, 2)),
            dma((4,)),
            dma((4, ZRING)),
            dma,
            dma((ROUNDS + 1, 2, 2)),
            dma((2, MESSAGES)),
            dma((2, MESSAGES)),
            dma((2,)),
        ],
        compiler_params=pltpu.CompilerParams(
            collective_id=0, has_side_effects=True, vmem_limit_bytes=58 * 2**20
        ),
    )(block_mask, queries.reshape(2, BLOCK, width), key_vectors, value_vectors)
    return turned.transpose(0, 2, 1).reshape(rows, width)


def solution(mesh):
    placed = (P("row", "col"), P(("col", "row"), None), P(("col", "row"), None), P())
    return jax.shard_map(body, mesh=mesh, in_specs=placed, out_specs=P("row", "col"), check_vma=False)
```

```python
import functools

import jax
import jax.numpy as jnp
from jax import lax
from jax.experimental import pallas as pl
from jax.experimental.pallas import tpu as pltpu
from jax.sharding import PartitionSpec as P

HEAD_DIM = 128
BLOCK = 512
SLOTS = 3
RING = 4
ZRING = 16
NSLOT = SLOTS * RING
PIECE = 128
HALF = 64
SUMROWS = 16
HERE = 8
LAST = 7
ROUNDS = 4
MESSAGES = 6
EARLY = 3
NEG_FILL = -1e30
NO_CAP = 3e38
EXP_SCALE = 1.4426950408889634 * HEAD_DIM**-0.5
MESH = pl.DeviceIdType.MESH
f32 = jnp.float32
bf16 = jnp.bfloat16


def dot(a, b, dims):
    return lax.dot_general(a, b, (dims, ((), ())), preferred_element_type=f32)


def kernel(
    mask_hbm,
    q_ref,
    k_ref,
    v_ref,
    o_ref,
    mask_ref,
    qg,
    kv,
    raw,
    scores,
    cap,
    near0,
    near1,
    state,
    maxima,
    osend,
    orecv,
    oin,
    ssend,
    srecv,
    sin,
    obuf,
    info_i,
    info_j,
    info_prev,
    info_diag,
    last,
    own_sem,
    near_sem,
    raw_sem,
    far_sem,
    q_sem,
    yb_send,
    yb_recv,
    z_send,
    z_recv,
    sib_send,
    sib_recv,
    o_sem,
    s_sem,
    out_sem,
):
    r = lax.axis_index("row")
    c = lax.axis_index("col")
    core = lax.rem(r, 2)
    zl = lax.rem(r // 2, RING)
    y = r // 8
    x = lax.rem(c, RING)
    z = (c // RING) * RING + zl
    parity, plane = lax.rem(y, 2), y // 2

    def at_x(d):
        return (r, (c // RING) * RING + lax.rem(x + d, RING))

    def at_y(d):
        return (lax.rem(y + d, RING) * 8 + lax.rem(r, 8), c)

    def at_z(d):
        t = lax.rem(z + d + ZRING, ZRING)
        return (y * 8 + lax.rem(t, RING) * 2 + core, (t // RING) * RING + x)

    sibling = (r + 1 - 2 * core, c)
    far = at_y(2)
    far_sibling = (far[0] + 1 - 2 * core, c)

    def remote(src, dst, send, recv, device):
        return pltpu.make_async_remote_copy(
            src_ref=src, dst_ref=dst, send_sem=send, recv_sem=recv, device_id=device, device_id_type=MESH
        )

    def drain(view, sem):
        pltpu.make_async_copy(view, view, sem).wait()

    own_k = pltpu.make_async_copy(k_ref, kv.at[HERE, parity, core, 0, plane], own_sem.at[0])
    own_v = pltpu.make_async_copy(v_ref, raw.at[0, core], own_sem.at[1])
    own_q = pltpu.make_async_copy(q_ref, qg.at[0], own_sem.at[2])
    own_mask = pltpu.make_async_copy(mask_hbm, mask_ref, own_sem.at[3])
    for copy in (own_k, own_v, own_q, own_mask):
        copy.start()

    barrier = pltpu.get_barrier_semaphore()
    partners = [sibling, far_sibling] + [at_z(d) for d in (1, -1, 2, -2)]
    partners += [at_x(d) for d in (1, 2, 3)] + [at_y(d) for d in (1, 2, 3)]
    for partner in partners:
        pl.semaphore_signal(barrier, inc=1, device_id=partner, device_id_type=MESH)
    pl.semaphore_wait(barrier, len(partners))

    first_copies = [
        remote(k_ref, kv.at[HERE, parity, core, 0, plane], far_sem.at[0], far_sem.at[1], far),
        remote(v_ref, raw.at[0, core], raw_sem.at[0, 0], raw_sem.at[1, 0], sibling),
        remote(v_ref, raw.at[1, core], raw_sem.at[0, 1], raw_sem.at[1, 1], far),
        remote(v_ref, raw.at[1, core], raw_sem.at[0, 2], raw_sem.at[1, 2], far_sibling),
    ]
    for copy in first_copies:
        copy.start()
    q_copies = [remote(q_ref, qg.at[RING - d], q_sem.at[0, d], q_sem.at[1, RING - d], at_x(d)) for d in (1, 2, 3)]
    for copy in q_copies:
        copy.start()

    def slab(stream, o):
        return kv.at[HERE + o, parity, core, stream % 2, plane if stream < 2 else 1 - plane]

    def send_z(stream, o, hop, source=None):
        remote(
            slab(stream, o) if source is None else source, slab(stream, o - hop), z_send.at[stream], z_recv.at[stream, HERE + o - hop], at_z(hop)
        ).start()

    def wait_z(stream, o):
        drain(slab(stream, o), z_recv.at[stream, HERE + o])

    def pieces(first, count, from_y):
        return kv.at[pl.ds(HERE + first, count), lax.rem(from_y, 2), core, :, from_y // 2]

    def spread(n, way, first, count):
        for d in (1, 3):
            view = pieces(first, count, y)
            remote(view, view, yb_send, yb_recv.at[n, way, d // 2], at_y(d)).start()

    def gathered(n, way, first, count):
        for d in (1, 3):
            drain(pieces(first, count, lax.rem(y + RING - d, RING)), yb_recv.at[n, way, d // 2])

    def shared(first, count, of_core, of_parity):
        return kv.at[pl.ds(HERE + first, count), of_parity, of_core]

    def share(n, way, first, count, part):
        view = shared(first, count, core, parity if part == 0 else 1 - parity)
        remote(view, view, sib_send, sib_recv.at[n, way, part], sibling).start()

    def arrivals(n):
        if n == 0:
            return [(0, 0, 1)]
        return [(0, -2 * n, 2), (1, 2 * n - 1, 2 if n < ROUNDS else 1)]

    for hop in (2, -2, 1, -1):
        send_z(0, 0, hop, k_ref)
    own_k.wait()
    own_v.wait()
    drain(raw.at[0, 1 - core], raw_sem.at[1, 0])
    own_turned = raw[0].reshape(PIECE, HEAD_DIM).astype(f32).T.astype(bf16)
    for i in (0, 1):

        @pl.when(core == i)
        def _():
            kv[HERE, parity, i, 1, plane] = own_turned[i * HALF : (i + 1) * HALF]

    for hop in (2, -2, 1, -1):
        send_z(1, 0, hop)
    drain(kv.at[HERE, parity, core, 0, 1 - plane], far_sem.at[1])
    for hop in (2, -2, 1, -1):
        send_z(2, 0, hop)
    drain(raw.at[1, core], raw_sem.at[1, 1])
    drain(raw.at[1, 1 - core], raw_sem.at[1, 2])
    far_turned = raw[1].reshape(PIECE, HEAD_DIM).astype(f32).T.astype(bf16)
    for i in (0, 1):

        @pl.when(core == i)
        def _():
            kv[HERE, parity, i, 1, 1 - plane] = far_turned[i * HALF : (i + 1) * HALF]

    for hop in (2, -2, 1, -1):
        send_z(3, 0, hop)
    spread(0, 0, 0, 1)
    share(0, 0, 0, 1, 0)

    zh = c // RING

    def valid(b):
        return b * RING + x <= r // 2

    def on_diagonal(b):
        return b * RING + x == r // 2

    side = jnp.where(zl < 2, 3, 1)
    third, fourth = lax.rem(zh + RING - side, RING), lax.rem(zh + 2, RING)
    order = [
        zh,
        lax.rem(zh + side, RING),
        jnp.where(valid(third), third, fourth),
        jnp.where(valid(third), fourth, third),
    ]
    n_late = valid(third).astype(jnp.int32) + valid(fourth).astype(jnp.int32)

    def prepare():
        for i in (0, 1):
            last[i] = jnp.int32(NSLOT)
        for place, b in enumerate(order):
            count = jnp.int32(0)
            found_i = [jnp.int32(0)] * SLOTS
            found_j = [jnp.int32(0)] * SLOTS
            for i in (0, 1):
                for j in range(RING):
                    flag = mask_ref[2 * r + i, (b * RING + x) * RING + j]
                    for s in range(SLOTS):
                        here = flag * jnp.where(count == s, 1, 0)
                        found_i[s] = found_i[s] + here * i
                        found_j[s] = found_j[s] + here * j
                    count = count + flag
            for s in range(SLOTS):
                t = place * SLOTS + s
                active = count > s
                i, j = found_i[s], found_j[s]
                info_i[t] = i
                info_j[t] = j
                info_prev[t] = jnp.where(i == 0, last[0], last[1])
                info_diag[t] = jnp.where(2 * r + i == (b * RING + x) * RING + j, 1, 0)
                last[0] = jnp.where(jnp.logical_and(active, i == 0), t, last[0])
                last[1] = jnp.where(jnp.logical_and(active, i == 1), t, last[1])
        key_at = lax.broadcasted_iota(jnp.int32, (BLOCK, BLOCK), 0)
        query_at = lax.broadcasted_iota(jnp.int32, (BLOCK, BLOCK), 1)
        cap[0] = jnp.full((BLOCK, BLOCK), NO_CAP, f32)
        cap[1] = jnp.where(key_at <= query_at, NO_CAP, NEG_FILL)
        for head in range(RING):
            state[head, NSLOT] = jnp.zeros(state.shape[2:], f32)
            maxima[head, NSLOT] = jnp.full(maxima.shape[2:], NEG_FILL, f32)

    ones = jnp.ones((SUMROWS, BLOCK), bf16)

    def at_place(place):
        return jnp.where(place == 1, order[1], jnp.where(place == 2, order[2], order[3]))

    def late_tile(kind, t, n):
        b = at_place(t // SLOTS)
        j = info_j[t]
        return kv[lax.rem(b * RING + n - z + HERE + ZRING, ZRING), lax.rem(j, 2), :, kind, j // 2]

    def near_tile(near):
        def tile(kind, t, n):
            j = info_j[t]
            return near[n, lax.rem(j, 2), :, kind, j // 2]

        return tile

    def score(tile, head, t):
        keys = jnp.concatenate([tile(0, t, n).reshape(PIECE, HEAD_DIM) for n in range(RING)], axis=0)
        return dot(keys, qg[head, info_i[t]], ((1,), (1,)))

    def soften(tile, head, t, s, masked):
        prev = info_prev[t]
        if masked:
            s = jnp.minimum(s, cap[info_diag[t]])
        old_max = maxima[head, prev]
        new_max = jnp.maximum(old_max, jnp.max(s, axis=0, keepdims=True))
        factor = jnp.exp2((old_max - new_max) * EXP_SCALE)
        weights = jnp.exp2((s - new_max) * EXP_SCALE).astype(bf16)
        values = jnp.concatenate([tile(1, t, n).reshape(PIECE, HEAD_DIM) for n in range(RING)], axis=1)
        values = jnp.concatenate([values, ones], axis=0)
        maxima[head, t] = new_max
        state[head, t] = state[head, prev] * factor + dot(values, weights, ((1,), (0,)))

    def stretch(tile, head, t, next_head, next_t, masked):
        for s in range(SLOTS):
            if s < SLOTS - 1:
                scores[s + 1] = score(tile, head, t + s + 1)
            else:
                scores[0] = score(tile, next_head, next_t)
            soften(tile, head, t + s, scores[s], masked)

    def head_of(n):
        return jnp.where(n == 0, 2, jnp.where(n == 1, 1, jnp.where(n == 2, 3, 0)))

    def early(near, place, count):
        tile, t = near_tile(near), place * SLOTS

        def heads(masked):
            scores[0] = score(tile, head_of(0), t)

            def head_body(n, carry):
                stretch(tile, head_of(n), t, head_of(n + 1), t, masked)
                return carry

            lax.fori_loop(0, count, head_body, 0)

        on = on_diagonal(order[place])
        pl.when(jnp.logical_and(valid(order[place]), jnp.logical_not(on)))(lambda: heads(False))
        pl.when(jnp.logical_and(valid(order[place]), on))(lambda: heads(True))

    def bring(near, place):
        first = lax.rem(order[place] * RING - z + HERE + ZRING, ZRING)
        return pltpu.make_async_copy(kv.at[pl.ds(first, RING)], near, near_sem.at[place])

    def wait_shared(n):
        for way, first, count in arrivals(n):
            drain(shared(first, count, 1 - core, parity), sib_recv.at[n, way, 0])
            drain(shared(first, count, 1 - core, 1 - parity), sib_recv.at[n, way, 1])

    for n in range(1, ROUNDS + 1):
        for hops in ((2, -2), (1, -1)):
            for stream in range(4):
                for hop in hops:
                    o = -2 * n if hop > 0 else 2 * n
                    if n < ROUNDS and abs(hop) == 2:
                        wait_z(stream, o)
                    if n < ROUNDS and o - hop <= LAST:
                        send_z(stream, o, hop)
        for way, first, count in arrivals(n):
            for o in range(first, first + count):
                if n == ROUNDS or abs(o) % 2:
                    wait_z(0, o)
                    wait_z(1, o)
            spread(n, way, first, count)
        for way, first, count in arrivals(n):
            for o in range(first, first + count):
                if n == ROUNDS or abs(o) % 2:
                    wait_z(2, o)
                    wait_z(3, o)
            share(n, way, first, count, 0)
        for way, first, count in arrivals(n - 1):
            gathered(n - 1, way, first, count)
            share(n - 1, way, first, count, 1)
        if n == 1:
            own_mask.wait()
            prepare()
        if n == ROUNDS - 1:
            own_q.wait()
            for d in (1, 2, 3):
                q_copies[d - 1].wait_recv()
            for m in range(n):
                wait_shared(m)
            copy = bring(near0, 0)
            copy.start()
            copy.wait()
    early(near0, 0, RING)
    for way, first, count in arrivals(ROUNDS):
        gathered(ROUNDS, way, first, count)
        share(ROUNDS, way, first, count, 1)
    wait_shared(ROUNDS - 1)
    copy = bring(near1, 1)
    copy.start()
    copy.wait()
    early(near1, 1, EARLY)
    wait_shared(ROUNDS)

    def message(m):
        head, i, to, into = (
            (2, 0, 1, oin.at[0]),
            (2, 1, 3, oin.at[1]),
            (1, 1, 1, orecv.at[0, 1]),
            (3, 0, 3, orecv.at[1, 0]),
            (1, 0, 1, orecv.at[0, 0]),
            (3, 1, 3, orecv.at[1, 1]),
        )[m]
        stats = (sin.at[0], sin.at[1], srecv.at[0, 1], srecv.at[1, 0], srecv.at[0, 0], srecv.at[1, 1])[m]
        return (
            remote(osend.at[head, i], into, o_sem.at[0, m], o_sem.at[1, m], at_x(to)),
            remote(ssend.at[head, i], stats, s_sem.at[0, m], s_sem.at[1, m], at_x(to)),
        )

    def send(*messages):
        for m in messages:
            for copy in message(m):
                copy.start()

    def arrived(*messages):
        for m in messages:
            for copy in message(m):
                copy.wait_recv()

    def merged(parts):
        tops = [stats[0:1] for _, stats in parts]
        top = functools.reduce(jnp.maximum, tops)
        shares = [jnp.exp2((a - top) * EXP_SCALE) for a in tops]
        total = sum(stats[1:2] * a for (_, stats), a in zip(parts, shares))
        return [p.astype(f32) for p, _ in parts], shares, top, total

    def first_of(n):
        return jnp.where(jnp.logical_and(n >= EARLY, valid(order[1])), 1, 2)

    scores[0] = score(late_tile, head_of(0), first_of(0) * SLOTS)

    def head_body(n, carry):
        head = head_of(n)

        @pl.when(n_late == 0)
        def _():
            scores[0] = score(late_tile, head, first_of(n) * SLOTS)

        def stretch_body(place, inner):
            done = place == n_late + 1
            slots = (
                late_tile,
                head,
                place * SLOTS,
                jnp.where(done, head_of(n + 1), head),
                jnp.where(done, first_of(n + 1), jnp.minimum(place + 1, RING - 1)) * SLOTS,
            )
            on = on_diagonal(at_place(place))
            pl.when(jnp.logical_not(on))(lambda: stretch(*slots, False))
            pl.when(on)(lambda: stretch(*slots, True))
            return inner

        lax.fori_loop(first_of(n), n_late + 2, stretch_body, 0)
        for i in (0, 1):
            final = state[head, last[i]]
            osend[head, i] = final[:HEAD_DIM].astype(bf16)
            ssend[head, i, 0:1] = maxima[head, last[i]]
            ssend[head, i, 1:2] = final[HEAD_DIM : HEAD_DIM + 1]

        @pl.when(n == 0)
        def _():
            send(0, 1)

        @pl.when(n == 1)
        def _():
            send(2)

        @pl.when(n == 2)
        def _():
            send(3)
            arrived(0, 1)
            for m, other, i in ((4, 1, 0), (5, 3, 1)):
                parts = [(osend[other, i], ssend[other, i]), (oin[i], sin[i])]
                values, shares, top, total = merged(parts)
                osend[other, i] = sum(p * a for p, a in zip(values, shares)).astype(bf16)
                ssend[other, i, 0:1] = top
                ssend[other, i, 1:2] = total
                send(m)

        return carry

    lax.fori_loop(0, RING, head_body, 0)
    outs = []
    for m, i in ((3, 0), (2, 1)):
        arrived(m)
        parts = [(osend[0, i], ssend[0, i]), (orecv[1 - i, i], srecv[1 - i, i])]
        values, shares, top, total = merged(parts)
        state[0, i, :HEAD_DIM] = sum(p * a for p, a in zip(values, shares))
        state[0, i, HEAD_DIM : HEAD_DIM + 1] = total
        maxima[0, i] = top
    for m, i in ((4, 0), (5, 1)):
        arrived(m)
        tops = [maxima[0, i], srecv[i, i, 0:1]]
        top = jnp.maximum(*tops)
        shares = [jnp.exp2((a - top) * EXP_SCALE) for a in tops]
        total = state[0, i, HEAD_DIM : HEAD_DIM + 1] * shares[0] + srecv[i, i, 1:2] * shares[1]
        shares = [a / total for a in shares]
        obuf[i] = (state[0, i, :HEAD_DIM] * shares[0] + orecv[i, i].astype(f32) * shares[1]).astype(bf16)
        outs.append(pltpu.make_async_copy(obuf.at[i], o_ref.at[i], out_sem.at[i]))
        outs[i].start()

    for d in (1, 2, 3):
        q_copies[d - 1].wait_send()
    for m in range(MESSAGES):
        for copy in message(m):
            copy.wait_send()
    for copy in first_copies:
        copy.wait_send()
    drain(kv.at[:, :, core, :, 0], yb_send)
    for stream in range(4):
        drain(kv.at[pl.ds(0, ZRING - 1), parity, core, 0, 0], z_send.at[stream])
    drain(kv.at[:, :, core], sib_send)
    for copy in outs:
        copy.wait()


def body(queries, key_vectors, value_vectors, block_mask):
    rows, width = queries.shape
    dma = pltpu.SemaphoreType.DMA
    turned = pl.pallas_call(
        kernel,
        out_shape=jax.ShapeDtypeStruct((2, width, BLOCK), bf16),
        in_specs=[pl.BlockSpec(memory_space=pltpu.HBM)] * 4,
        out_specs=pl.BlockSpec(memory_space=pltpu.HBM),
        scratch_shapes=[
            pltpu.SMEM(block_mask.shape, jnp.int32),
            pltpu.VMEM((RING, 2, BLOCK, HEAD_DIM), bf16),
            pltpu.VMEM((ZRING, 2, 2, 2, 2, HALF, HEAD_DIM), bf16),
            pltpu.VMEM((2, 2, HALF, HEAD_DIM), bf16),
            pltpu.VMEM((SLOTS, BLOCK, BLOCK), f32),
            pltpu.VMEM((2, BLOCK, BLOCK), f32),
            pltpu.VMEM((RING, 2, 2, 2, 2, HALF, HEAD_DIM), bf16),
            pltpu.VMEM((RING, 2, 2, 2, 2, HALF, HEAD_DIM), bf16),
            pltpu.VMEM((RING, NSLOT + 1, HEAD_DIM + SUMROWS, BLOCK), f32),
            pltpu.VMEM((RING, NSLOT + 1, 1, BLOCK), f32),
            pltpu.VMEM((RING, 2, HEAD_DIM, BLOCK), bf16),
            pltpu.VMEM((2, 2, HEAD_DIM, BLOCK), bf16),
            pltpu.VMEM((2, HEAD_DIM, BLOCK), bf16),
            pltpu.VMEM((RING, 2, 8, BLOCK), f32),
            pltpu.VMEM((2, 2, 8, BLOCK), f32),
            pltpu.VMEM((2, 8, BLOCK), f32),
            pltpu.VMEM((2, HEAD_DIM, BLOCK), bf16),
            pltpu.SMEM((NSLOT,), jnp.int32),
            pltpu.SMEM((NSLOT,), jnp.int32),
            pltpu.SMEM((NSLOT,), jnp.int32),
            pltpu.SMEM((NSLOT,), jnp.int32),
            pltpu.SMEM((2,), jnp.int32),
            dma((4,)),
            dma((2,)),
            dma((2, 3)),
            dma((2,)),
            dma((2, RING)),
            dma,
            dma((ROUNDS + 1, 2, 2)),
            dma((4,)),
            dma((4, ZRING)),
            dma,
            dma((ROUNDS + 1, 2, 2)),
            dma((2, MESSAGES)),
            dma((2, MESSAGES)),
            dma((2,)),
        ],
        compiler_params=pltpu.CompilerParams(
            collective_id=0, has_side_effects=True, vmem_limit_bytes=58 * 2**20
        ),
    )(block_mask, queries.reshape(2, BLOCK, width), key_vectors, value_vectors)
    return turned.transpose(0, 2, 1).reshape(rows, width)


def solution(mesh):
    placed = (P("row", "col"), P(("col", "row"), None), P(("col", "row"), None), P())
    return jax.shard_map(body, mesh=mesh, in_specs=placed, out_specs=P("row", "col"), check_vma=False)
```
